512 devices in a mesh: pipe: 4 (over y_hi, core), seq: 32 (over y_lo, z), dp: 4 (over x).
Axes of the slice: x: 4, y: 8 (y_hi: 2, y_lo: 4; y = y_hi * 4 + y_lo), z: 8, core: 2. Of those that a mesh axis runs over, the one named last changes fastest.
Arguments:
- clips_in: bfloat16 [8, 128, 5120], P('dp', None, 'seq'), may hold values from -6 to 6
- action_ids: int32 [8, 8], P('dp'), may hold values from 0 to 7
- frame_visible: int32 [8, 8], P('dp'), may hold values 0 or 1
- plan: int32 [2], replicated, may hold values from 0 to 1, each once
- qkv_weight: bfloat16 [4, 5120, 12288], P('pipe', None, 'seq'), may hold values from -0.08385255 to 0.08385255
- norm_gain: bfloat16 [4, 5120], P('pipe'), may hold values from 0.25 to 1.75
- action_table: bfloat16 [4, 8, 5120], P('pipe', None, 'seq'), may hold values from -3 to 3
- out_weight: bfloat16 [4, 4096, 5120], P('pipe', 'dp', 'seq'), may hold values from -0.09375 to 0.09375
Outputs:
- section_out: bfloat16 [4, 8, 128, 5120], P('pipe', 'dp', None, 'seq')
The draws below stay inside these ranges and needn't reach their ends.
Inputs may be any that keep to these rules, and one draw needn't show every extreme that they name: `plan`: a permutation of 0 to 1.
All inputs are finite; a program needn't handle non-finite values. No bound on the sum of `frame_visible` on one device may be relied on, other than what follows from the above.
Results may differ from the reference program's by a relative error of at most 0.02.
Values may be sent and summed in bfloat16 or wider, within the bound.
A program may use at most 64 MiB of HBM per device.

```python
import jax
import jax.numpy as jnp
from jax import lax

D = 5120
HEADS = 32
HD = 128
NACT = 8
FRAMES = 8
SPATIAL = 16
MB = 2
TOK = 128
SECTIONS = 4
CLIPS = 8
N_DP = 4


def draw_qkv_weight(key, part):
    key = jax.random.fold_in(key, 11)
    spread = D ** (-0.5)
    limit = 5.9 * spread
    base_key = jax.random.fold_in(key, 0)
    shape = (SECTIONS, D, HEADS, 3, HD)
    values = jnp.clip(jax.random.normal(base_key, shape, jnp.float32) * spread, -limit, limit)
    return values.reshape(SECTIONS, D, HEADS * 3 * HD).astype(jnp.bfloat16)


def with_ends(values, key, smallest, high):
    longest = values.shape.index(max(values.shape))
    spots = []
    for shift in (0, 1):
        where = [jax.random.randint(jax.random.fold_in(key, axis), (), 0, length) for axis, length in enumerate(values.shape)]
        where[longest] = (where[longest] + shift) % values.shape[longest]
        spots.append(tuple(where))
    return values.at[spots[0]].set(smallest).at[spots[1]].set(high)


def block_scale(key, extent, shards, least, largest):
    level = 1.0
    for axis_at, parts in shards:
        draws = jax.random.uniform(jax.random.fold_in(jax.random.fold_in(key, 6), axis_at), (parts,), jnp.float32, least / len(shards), largest / len(shards))
        level = level * jnp.repeat(jnp.exp(draws), extent[axis_at] // parts).reshape((-1,) + (1,) * (len(extent) - 1 - axis_at))
    return level


def centred(stream_key, extent, width, most, pieces=(), held_as=jnp.bfloat16):
    drawn = width * jax.random.normal(stream_key, extent, jnp.float32)
    if pieces:
        drawn = drawn * block_scale(stream_key, extent, pieces, -0.22, 0.18)
    return jnp.clip(drawn, -most, most).astype(held_as)


def setup_inputs(seed: int = 0) -> dict:
    splits = jax.random.split(jax.random.key(seed), 9)
    return {
        "clips_in": centred(splits[0], (CLIPS, TOK, D), 1.0, 6.0, ((0, 4), (2, 32))),
        "action_ids": with_ends(jax.random.randint(splits[1], (CLIPS, FRAMES), 0, NACT), jax.random.fold_in(splits[1], 1), 0, NACT - 1).astype(jnp.int32),
        "frame_visible": with_ends((jax.random.randint(splits[2], (CLIPS, FRAMES), 0, 4) < 3).astype(jnp.int32), jax.random.fold_in(splits[2], 1), 0, 1),
        "plan": jax.random.permutation(splits[3], MB).astype(jnp.int32),
        "qkv_weight": draw_qkv_weight(jax.random.fold_in(splits[8], 71), 0),
        "norm_gain": jnp.clip(1.0 + 0.15 * jax.random.normal(splits[5], (SECTIONS, D), jnp.float32), 0.25, 1.75).astype(jnp.bfloat16),
        "action_table": centred(splits[6], (SECTIONS, NACT, D), 0.5, 3.0, ((0, 4), (2, 32))),
        "out_weight": centred(splits[7], (SECTIONS, HEADS * HD, D), (HEADS * HD) ** -0.5, 0.09375, ((0, 4), (1, 4), (2, 32))),
    }


def layer_step(h_in, acts, visible, wqkv, gain, table, wout, parity):
    frame = jnp.arange(TOK, dtype=jnp.int32) // SPATIAL
    place = jnp.arange(TOK, dtype=jnp.int32) % SPATIAL
    onehot = (acts[frame][:, None] == jnp.arange(NACT, dtype=jnp.int32)[None, :]).astype(jnp.bfloat16)
    embed = jnp.dot(onehot, table, preferred_element_type=jnp.float32)
    cond = (h_in.astype(jnp.float32) + embed).astype(jnp.bfloat16)
    condf = cond.astype(jnp.float32)
    scale = jax.lax.rsqrt(lax.optimization_barrier(jnp.mean(condf * condf, axis=-1)) + 1e-05)
    normed = (condf * scale[:, None] * gain.astype(jnp.float32)).astype(jnp.bfloat16)
    qkv = jnp.dot(normed, wqkv, preferred_element_type=jnp.float32).astype(jnp.bfloat16)
    qkv = qkv.reshape(TOK, HEADS, 3, HD).astype(jnp.float32)
    query, keys, values = (qkv[:, :, 0], qkv[:, :, 1], qkv[:, :, 2])
    scores = jnp.einsum('qhd,khd->hqk', query, keys) * HD ** (-0.5)
    same_frame = frame[:, None] == frame[None, :]
    own_frame = frame[None, :] == frame[:, None]
    seen = (visible[frame][None, :] == 1) | own_frame
    temporal = (place[:, None] == place[None, :]) & (frame[None, :] <= frame[:, None]) & seen
    allowed = same_frame if parity == 0 else temporal
    scores = jnp.where(allowed[None], scores, -1e+30)
    top = lax.optimization_barrier(jnp.max(scores, axis=-1, keepdims=True))
    weights = jnp.exp(scores - top)
    probs = (weights / lax.optimization_barrier(jnp.sum(weights, axis=-1, keepdims=True))).astype(jnp.bfloat16)
    attn = jnp.einsum('hqk,khd->qhd', probs.astype(jnp.float32), values).astype(jnp.bfloat16)
    attn = attn.reshape(TOK, HEADS * HD)
    proj = jnp.dot(attn, wout, preferred_element_type=jnp.float32)
    return (condf + proj).astype(jnp.bfloat16)

def reference(clips_in, action_ids, frame_visible, plan, qkv_weight, norm_gain, action_table, out_weight):
    results = jnp.zeros((SECTIONS, CLIPS, TOK, D), jnp.bfloat16)
    for group in range(N_DP):
        for slot in range(MB):
            clip = group * MB + plan[slot]
            stream = clips_in[clip]
            for layer in range(SECTIONS):
                stream = layer_step(stream, action_ids[clip], frame_visible[clip], qkv_weight[layer], norm_gain[layer], action_table[layer], out_weight[layer], layer % 2)
                results = results.at[layer, group * MB + slot].set(stream)
    return results
```

```python
import functools

import jax
import jax.numpy as jnp
from jax import lax
from jax.experimental import pallas as pl
from jax.experimental.pallas import tpu as pltpu
from jax.sharding import PartitionSpec as P

HD = 128
SPATIAL = 16
FRAMES = 8
NY = 4
NZ = 8
MESH = pl.DeviceIdType.MESH


def kernel(
    plan, acts, vis,
    clips, table, wq, wo_loc,
    out,
    xbuf, abuf, wo, hin, acc, proj,
    ysend, yrecv, zsend, zrecv, dsend, drecv, psend, precv, lsem,
):
    p = lax.axis_index("pipe")
    s = lax.axis_index("seq")
    d = lax.axis_index("dp")
    y = s // NZ
    z = s % NZ
    f = hin.shape[0]
    toks = hin.shape[1] // 2

    def seq_id(yy, zz):
        return {"seq": yy * NZ + zz}

    peers_y = [seq_id((y + k) % NY, z) for k in range(1, NY)]
    z_right = seq_id(y, (z + 1) % NZ)
    z_left = seq_id(y, (z + NZ - 1) % NZ)
    peers_d = [{"dp": (d + k) % 4} for k in range(1, 4)]
    p_next = {"pipe": (p + 1) % 4}
    p_prev = {"pipe": (p + 3) % 4}

    barrier = pltpu.get_barrier_semaphore()
    everyone = peers_y + [z_right, z_left] + peers_d + [p_next, p_prev]
    for peer in everyone:
        pl.semaphore_signal(barrier, inc=1, device_id=peer, device_id_type=MESH)
    pl.semaphore_wait(barrier, len(everyone))

    wo_copies = []
    wo_mine = wo.at[:, :, pl.ds(pl.multiple_of(d * HD, HD), HD)]
    own_copy = pltpu.make_async_copy(wo_loc, wo_mine, lsem)
    own_copy.start()
    for k in range(3):
        c = pltpu.make_async_remote_copy(
            src_ref=wo_loc, dst_ref=wo_mine,
            send_sem=dsend.at[k], recv_sem=drecv.at[k],
            device_id=peers_d[k], device_id_type=MESH,
        )
        c.start()
        wo_copies.append(c)

    pipe_copy = pltpu.make_async_remote_copy(
        src_ref=out, dst_ref=hin,
        send_sem=psend, recv_sem=precv,
        device_id=p_next, device_id_type=MESH,
    )

    @pl.when(p == 0)
    def _():
        for j in range(2):
            hin[:, j * toks:(j + 1) * toks] = clips[plan[j]]

    rows8 = lax.broadcasted_iota(jnp.int32, (8, 2 * toks), 0)
    lane = lax.broadcasted_iota(jnp.int32, (8, 2 * toks), 1)
    act_of = jnp.zeros((8, 2 * toks), jnp.int32)
    for j in range(2):
        for fr in range(FRAMES):
            act_of = jnp.where(lane // SPATIAL == j * FRAMES + fr, acts[plan[j], fr], act_of)
    onehot = (act_of == rows8).astype(jnp.float32)
    embed = lax.dot_general(
        table[...].astype(jnp.float32), onehot, (((0,), (0,)), ((), ())),
        preferred_element_type=jnp.float32, precision=lax.Precision.HIGHEST,
    )

    @pl.when(p > 0)
    def _():
        pipe_copy.wait_recv()

    def gather(g, buf, r, use):
        own = buf.at[pl.ds(pl.multiple_of((z * NY + y) * r, r), r), :]
        copies = []
        for k in range(NY - 1):
            c = pltpu.make_async_remote_copy(
                src_ref=own, dst_ref=own,
                send_sem=ysend.at[g, k], recv_sem=yrecv.at[g, k],
                device_id=peers_y[k], device_id_type=MESH,
            )
            c.start()
            copies.append(c)
        for c in copies:
            c.wait_recv()

        def part(col, h):
            return buf.at[pl.ds(pl.multiple_of((col * NY + 2 * h) * r, r), 2 * r), :]

        ring = {}
        for i in range(NZ // 2):
            c_right = (z + NZ - i) % NZ
            c_left = (z + i) % NZ
            for h in range(2):
                for way, col, peer in ((0, c_right, z_right), (1, c_left, z_left)):
                    if i > 0:
                        ring[way, i - 1, h].wait_recv()
                    if i == NZ // 2 - 1 and way != h:
                        continue
                    c = pltpu.make_async_remote_copy(
                        src_ref=part(col, h), dst_ref=part(col, h),
                        send_sem=zsend.at[g, way, i, h], recv_sem=zrecv.at[g, way, i, h],
                        device_id=peer, device_id_type=MESH,
                    )
                    c.start()
                    ring[way, i, h] = c
                    copies.append(c)
            use(c_right)
            if i > 0:
                use(c_left)
        last = NZ // 2 - 1
        ring[0, last, 0].wait_recv()
        ring[1, last, 1].wait_recv()
        use((z + NZ // 2) % NZ)
        return copies

    own_f = pl.ds(pl.multiple_of((z * NY + y) * f, f), f)
    xbuf[own_f, :] = (hin[...].astype(jnp.float32) + embed).astype(jnp.bfloat16)
    acc[...] = jnp.zeros_like(acc)
    square = [jnp.zeros((1, 2 * toks), jnp.float32)]

    def use_cond(col):
        x = xbuf[pl.ds(pl.multiple_of(col * NY * f, NY * f), NY * f), :]
        acc[...] += jnp.dot(wq[col], x, preferred_element_type=jnp.float32)
        xf = x.astype(jnp.float32)
        square[0] += jnp.sum(xf * xf, axis=0, keepdims=True)

    sent = gather(0, xbuf, f, use_cond)
    scale = lax.rsqrt(square[0] * (1.0 / (NY * NZ * f)) + 1e-05)

    kpos = lax.broadcasted_iota(jnp.int32, (toks, toks), 0)
    qpos = lax.broadcasted_iota(jnp.int32, (toks, toks), 1)
    kframe, qframe = kpos // SPATIAL, qpos // SPATIAL
    same_frame = kframe == qframe
    causal = (kpos % SPATIAL == qpos % SPATIAL) & (kframe <= qframe)
    even = p % 2 == 0
    own_a = pl.ds(pl.multiple_of((z * NY + y) * HD, HD), HD)
    for j in range(2):
        seen = jnp.zeros((toks, toks), jnp.int32)
        for fr in range(FRAMES):
            seen = jnp.where(kframe == fr, vis[plan[j], fr], seen)
        temporal = jnp.where(causal & ((seen == 1) | same_frame), 1, 0)
        allowed = jnp.where(even, jnp.where(same_frame, 1, 0), temporal)
        cols = slice(j * toks, (j + 1) * toks)
        qkv = (acc[:, cols] * scale[:, cols]).astype(jnp.bfloat16)
        query, keys, values = qkv[:HD], qkv[HD:2 * HD], qkv[2 * HD:]
        scores = lax.dot_general(
            keys, query, (((0,), (0,)), ((), ())), preferred_element_type=jnp.float32
        ) * HD ** (-0.5)
        scores = jnp.where(allowed == 1, scores, -1e30)
        top = jnp.max(scores, axis=0, keepdims=True)
        weights = jnp.exp(scores - top)
        probs = (weights / jnp.sum(weights, axis=0, keepdims=True)).astype(jnp.bfloat16)
        attn = jnp.dot(values, probs, preferred_element_type=jnp.float32)
        abuf[own_a, cols] = attn.astype(jnp.bfloat16)

    for c in wo_copies:
        c.wait_recv()
    own_copy.wait()
    proj[...] = xbuf[own_f, :].astype(jnp.float32)

    def use_attn(col):
        a = abuf[pl.ds(pl.multiple_of(col * NY * HD, NY * HD), NY * HD), :]
        proj[...] += jnp.dot(wo[col], a, preferred_element_type=jnp.float32)

    sent += gather(1, abuf, HD, use_attn)
    out[...] = proj[...].astype(jnp.bfloat16)

    @pl.when(p < 3)
    def _():
        pipe_copy.start()
        pipe_copy.wait_send()

    for c in sent + wo_copies:
        c.wait_send()


def shards(
    clips_in, action_ids, frame_visible, plan, qkv_weight, norm_gain, action_table, out_weight
):
    clips, toks, f = clips_in.shape
    n = qkv_weight.shape[2]
    bf16 = jnp.bfloat16
    xt = jnp.swapaxes(clips_in, 1, 2)
    wq = (qkv_weight[0].astype(jnp.float32) * norm_gain[0].astype(jnp.float32)[:, None]).astype(bf16)
    wq = wq.reshape(NY, NZ, f, n).transpose(1, 3, 0, 2).reshape(NZ, n, NY * f)
    wo_loc = out_weight[0].reshape(NZ, HD, f).transpose(0, 2, 1)
    smem = pl.BlockSpec(memory_space=pltpu.SMEM)
    vmem = pl.BlockSpec(memory_space=pltpu.VMEM)
    dma = pltpu.SemaphoreType.DMA
    res = pl.pallas_call(
        kernel,
        out_shape=jax.ShapeDtypeStruct((f, 2 * toks), bf16),
        in_specs=[smem] * 3 + [vmem] * 4,
        out_specs=vmem,
        scratch_shapes=[
            pltpu.VMEM((NY * NZ * f, 2 * toks), bf16),
            pltpu.VMEM((NY * NZ * HD, 2 * toks), bf16),
            pltpu.VMEM((NZ, f, NY * HD), bf16),
            pltpu.VMEM((f, 2 * toks), bf16),
            pltpu.VMEM((n, 2 * toks), jnp.float32),
            pltpu.VMEM((f, 2 * toks), jnp.float32),
            dma((2, 3)), dma((2, 3)),
            dma((2, 2, 4, 2)), dma((2, 2, 4, 2)),
            dma((3,)), dma((3,)),
            dma, dma, dma,
        ],
        compiler_params=pltpu.CompilerParams(
            collective_id=0, has_side_effects=True, vmem_limit_bytes=48 * 1024 * 1024
        ),
    )(plan, action_ids, frame_visible, xt, action_table[0], wq, wo_loc)
    return res.reshape(f, clips, toks).transpose(1, 2, 0)[None]


def solution(mesh):
    return jax.shard_map(
        shards,
        mesh=mesh,
        in_specs=(
            P("dp", None, "seq"),
            P("dp", None),
            P("dp", None),
            P(),
            P("pipe", None, "seq"),
            P("pipe", None),
            P("pipe", None, "seq"),
            P("pipe", "dp", "seq"),
        ),
        out_specs=P("pipe", "dp", None, "seq"),
        check_vma=False,
    )
```

```python
import jax
import jax.numpy as jnp
from jax import lax
from jax.experimental import pallas as pl
from jax.experimental.pallas import tpu as pltpu
from jax.sharding import PartitionSpec as P

HD = 128
SPATIAL = 16
FRAMES = 8
NY = 4
NZ = 8
MESH = pl.DeviceIdType.MESH


def kernel(
    plan, acts, vis,
    clips, table, wq, wo_loc,
    out,
    xbuf, abuf, wo, hin, acc, pacc, pbuf, rbuf,
    ysend, yrecv, zsend, zrecv, asend, arecv, rsend, rrecv, psend, precv, wsend, wrecv, go,
):
    p = lax.axis_index("pipe")
    s = lax.axis_index("seq")
    d = lax.axis_index("dp")
    y = s // NZ
    z = s % NZ
    f, toks = hin.shape[1], hin.shape[2]
    sends = []

    def place(yy, zz):
        return {"seq": (yy % NY) * NZ + zz % NZ}

    def remote(src, dst, send_sem, recv_sem, device):
        return pltpu.make_async_remote_copy(
            src_ref=src, dst_ref=dst, send_sem=send_sem, recv_sem=recv_sem,
            device_id=device, device_id_type=MESH,
        )

    def greet(device):
        pl.semaphore_signal(barrier, inc=1, device_id=device, device_id_type=MESH)

    own_wo = jnp.where(y == d, 1, 0)
    barrier = pltpu.get_barrier_semaphore()
    for k in range(1, NY):
        greet(place(y + k, z))
    for k in range(1, NZ):
        greet(place(y, z + k))
    greet({"pipe": (p + 1) % 4})
    greet({"pipe": (p + 3) % 4})
    for k in range(NY):
        @pl.when((y != d) | (y != k))
        def _():
            greet({"dp": y, "seq": k * NZ + z})

    pl.semaphore_wait(barrier, NY - 1 + NZ - 1 + 2 + NY - own_wo)

    wo_here = [
        remote(wo_loc, wo.at[y], wsend.at[k], wrecv.at[y],
               {"dp": (d + k) % NY, "seq": d * NZ + z})
        for k in range(NY)
    ]
    wo_self = pltpu.make_async_copy(wo_loc, wo.at[y], wrecv.at[y])

    def start_wo():
        for k in range(1, NY):
            wo_here[k].start()

        @pl.when(y == d)
        def _():
            wo_self.start()

        @pl.when(y != d)
        def _():
            wo_here[0].start()

    def wait_wo():
        for k in range(NY):
            pltpu.make_async_copy(wo_loc, wo.at[k], wrecv.at[k]).wait()

    @pl.when(p == 1)
    def _():
        pl.semaphore_wait(go, 1)

    @pl.when(p > 0)
    def _():
        start_wo()

    rows8 = lax.broadcasted_iota(jnp.int32, (8, toks), 0)
    lane = lax.broadcasted_iota(jnp.int32, (8, toks), 1)

    def embed(j):
        act_of = jnp.zeros((8, toks), jnp.int32)
        for fr in range(FRAMES):
            act_of = jnp.where(lane // SPATIAL == fr, acts[plan[j], fr], act_of)
        onehot = (act_of == rows8).astype(jnp.float32)
        return lax.dot_general(
            table[...].astype(jnp.float32), onehot, (((0,), (0,)), ((), ())),
            preferred_element_type=jnp.float32, precision=lax.Precision.HIGHEST,
        )

    embeds = [embed(j) for j in range(2)]
    pipe_copies = [
        remote(out.at[j], hin.at[j], psend.at[j], precv.at[j], {"pipe": (p + 1) % 4})
        for j in range(2)
    ]
    own_f = pl.ds(pl.multiple_of((z * NY + y) * f, f), f)

    def block(j, yy, zz):
        row = ((zz + NZ) % NZ * NY + (yy + NY) % NY) * f
        return xbuf.at[j, pl.ds(pl.multiple_of(row, f), f), :]

    ring = {}

    def ring_send(j, way, i, k):
        ref = block(j, y - k, z + i if way else z - i)
        c = remote(ref, ref, zsend.at[j, way, i, k], zrecv.at[j, way, i, k],
                   place(y, z + NZ - 1 if way else z + 1))
        c.start()
        ring[j, way, i, k] = c
        sends.append(c)

    ycopies = {}

    def cond(j):
        @pl.when(p == 0)
        def _():
            hin[j] = clips[plan[j]]

        @pl.when(p > 0)
        def _():
            pipe_copies[j].wait_recv()

        xbuf[j, own_f, :] = (hin[j].astype(jnp.float32) + embeds[j]).astype(jnp.bfloat16)
        for k in range(1, NY):
            ref = block(j, y, z)
            c = remote(ref, ref, ysend.at[j, k - 1], yrecv.at[j, k - 1], place(y + k, z))
            c.start()
            ycopies[j, k] = c
            sends.append(c)
        for way in range(2):
            ring_send(j, way, 0, 0)
        acc[j] = jnp.zeros_like(acc[j])

    square = [jnp.zeros((1, toks), jnp.float32) for _ in range(2)]

    def use(j, zz):
        col = (zz + NZ) % NZ
        x = xbuf[j, pl.ds(pl.multiple_of(col * NY * f, NY * f), NY * f), :]
        acc[j] += jnp.dot(wq[col], x, preferred_element_type=jnp.float32)
        xf = x.astype(jnp.float32)
        square[j] += jnp.sum(xf * xf, axis=0, keepdims=True)

    def xstage(j, i):
        if i == 0:
            for k in range(1, NY):
                ycopies[j, k].wait_recv()
                for way in range(2):
                    ring_send(j, way, 0, k)
            use(j, z)
            return
        for k in range(NY):
            for way in range(2):
                if (j, way, i - 1, k) in ring:
                    ring[j, way, i - 1, k].wait_recv()
                    if i < 3 or (i == 3 and (k < 2) == (way == 0)):
                        ring_send(j, way, i, k)
        use(j, z - i)
        if i < 4:
            use(j, z + i)

    kpos = lax.broadcasted_iota(jnp.int32, (toks, toks), 0)
    qpos = lax.broadcasted_iota(jnp.int32, (toks, toks), 1)
    kframe, qframe = kpos // SPATIAL, qpos // SPATIAL
    acopies = {}

    def attention(j):
        same_frame = kframe == qframe
        causal = (kpos % SPATIAL == qpos % SPATIAL) & (kframe <= qframe)
        seen = jnp.zeros((toks, toks), jnp.int32)
        for fr in range(FRAMES):
            seen = jnp.where(kframe == fr, vis[plan[j], fr], seen)
        temporal = jnp.where(causal & ((seen == 1) | same_frame), 1, 0)
        allowed = jnp.where(p % 2 == 0, jnp.where(same_frame, 1, 0), temporal)
        scale = lax.rsqrt(square[j] * (1.0 / (NY * NZ * f)) + 1e-05)
        qkv = (acc[j] * scale).astype(jnp.bfloat16)
        query, keys, values = qkv[:HD], qkv[HD:2 * HD], qkv[2 * HD:]
        scores = lax.dot_general(
            keys, query, (((0,), (0,)), ((), ())), preferred_element_type=jnp.float32
        ) * HD ** (-0.5)
        scores = jnp.where(allowed == 1, scores, -1e30)
        top = jnp.max(scores, axis=0, keepdims=True)
        weights = jnp.exp(scores - top)
        probs = (weights / jnp.sum(weights, axis=0, keepdims=True)).astype(jnp.bfloat16)
        attn = jnp.dot(values, probs, preferred_element_type=jnp.float32)
        own_a = pl.ds(pl.multiple_of(z * HD, HD), HD)
        abuf[j, own_a, :] = attn.astype(jnp.bfloat16)
        for k in (4, 3, 5, 2, 6, 1, 7):
            ref = abuf.at[j, own_a, :]
            c = remote(ref, ref, asend.at[j, k - 1], arecv.at[j, k - 1], place(y, z + k))
            c.start()
            acopies[j, k] = c
            sends.append(c)

    rcopies = {}

    def project(j):
        for k in range(1, NZ):
            acopies[j, k].wait_recv()
        for yy in range(NY):
            part = jnp.dot(wo[yy], abuf[j], preferred_element_type=jnp.float32)
            pacc[j, yy] = part
            pbuf[j, yy] = part.astype(jnp.bfloat16)
        for k in (2, 1, 3):
            c = remote(pbuf.at[j, (y + k) % NY], rbuf.at[j, k - 1],
                       rsend.at[j, k - 1], rrecv.at[j, k - 1], place(y + k, z))
            c.start()
            rcopies[j, k] = c
            sends.append(c)

    def finish(j):
        total = pacc[j, y]
        for k in range(1, NY):
            rcopies[j, k].wait_recv()
            total += rbuf[j, k - 1].astype(jnp.float32)
        out[j] = (xbuf[j, own_f, :].astype(jnp.float32) + total).astype(jnp.bfloat16)

        @pl.when(p < 3)
        def _():
            pipe_copies[j].start()

    cond(0)
    xstage(0, 0)

    @pl.when(p == 0)
    def _():
        start_wo()

    for i in range(1, 5):
        xstage(0, i)
    cond(1)
    attention(0)
    xstage(1, 0)
    xstage(1, 1)
    wait_wo()

    @pl.when(p == 0)
    def _():
        pl.semaphore_signal(go, inc=1, device_id={"pipe": 1}, device_id_type=MESH)

    project(0)
    xstage(1, 2)
    xstage(1, 3)
    finish(0)
    xstage(1, 4)
    attention(1)
    project(1)
    finish(1)

    for c in sends + wo_here[1:]:
        c.wait_send()

    @pl.when(y != d)
    def _():
        wo_here[0].wait_send()

    @pl.when(p < 3)
    def _():
        for c in pipe_copies:
            c.wait_send()


def shards(
    clips_in, action_ids, frame_visible, plan, qkv_weight, norm_gain, action_table, out_weight
):
    clips, toks, f = clips_in.shape
    n = qkv_weight.shape[2]
    rows = out_weight.shape[1]
    bf16 = jnp.bfloat16
    xt = jnp.swapaxes(clips_in, 1, 2)
    wq = (qkv_weight[0].astype(jnp.float32) * norm_gain[0].astype(jnp.float32)[:, None]).astype(bf16)
    wq = wq.reshape(NY, NZ, f, n).transpose(1, 3, 0, 2).reshape(NZ, n, NY * f)
    wo_loc = out_weight[0].T
    smem = pl.BlockSpec(memory_space=pltpu.SMEM)
    vmem = pl.BlockSpec(memory_space=pltpu.VMEM)
    dma = pltpu.SemaphoreType.DMA
    res = pl.pallas_call(
        kernel,
        out_shape=jax.ShapeDtypeStruct((clips, f, toks), bf16),
        in_specs=[smem] * 3 + [vmem] * 4,
        out_specs=vmem,
        scratch_shapes=[
            pltpu.VMEM((clips, NY * NZ * f, toks), bf16),
            pltpu.VMEM((clips, NZ * HD, toks), bf16),
            pltpu.VMEM((NY, f, rows), bf16),
            pltpu.VMEM((clips, f, toks), bf16),
            pltpu.VMEM((clips, n, toks), jnp.float32),
            pltpu.VMEM((clips, NY, f, toks), jnp.float32),
            pltpu.VMEM((clips, NY, f, toks), bf16),
            pltpu.VMEM((clips, NY - 1, f, toks), bf16),
            dma((2, 3)), dma((2, 3)),
            dma((2, 2, 4, 4)), dma((2, 2, 4, 4)),
            dma((2, 7)), dma((2, 7)),
            dma((2, 3)), dma((2, 3)),
            dma((2,)), dma((2,)),
            dma((4,)), dma((4,)),
            pltpu.SemaphoreType.REGULAR,
        ],
        compiler_params=pltpu.CompilerParams(
            collective_id=0, has_side_effects=True, vmem_limit_bytes=48 * 1024 * 1024
        ),
    )(plan, action_ids, frame_visible, xt, action_table[0], wq, wo_loc)
    return jnp.swapaxes(res, 1, 2)[None]


def solution(mesh):
    return jax.shard_map(
        shards,
        mesh=mesh,
        in_specs=(
            P("dp", None, "seq"),
            P("dp", None),
            P("dp", None),
            P(),
            P("pipe", None, "seq"),
            P("pipe", None),
            P("pipe", None, "seq"),
            P("pipe", "dp", "seq"),
        ),
        out_specs=P("pipe", "dp", None, "seq"),
        check_vma=False,
    )
```

```python
import jax
import jax.numpy as jnp
from jax import lax
from jax.experimental import pallas as pl
from jax.experimental.pallas import tpu as pltpu
from jax.sharding import PartitionSpec as P

HD = 128
SPATIAL = 16
FRAMES = 8
NY = 4
NZ = 8
MESH = pl.DeviceIdType.MESH


def kernel(
    plan, acts, vis,
    clips, table, wq, wo_loc,
    out,
    xbuf, abuf, wx, wo, hin, acc, pacc, pbuf, rbuf,
    ysend, yrecv, zsend, zrecv, asend, arecv, rsend, rrecv, psend, precv,
    dsend, drecv, wsend, wrecv, lsem, go,
):
    p = lax.axis_index("pipe")
    s = lax.axis_index("seq")
    d = lax.axis_index("dp")
    y = s // NZ
    z = s % NZ
    f, toks = hin.shape[1], hin.shape[2]
    sends = []

    def place(yy, zz):
        return {"seq": (yy % NY) * NZ + zz % NZ}

    def remote(src, dst, send_sem, recv_sem, device):
        return pltpu.make_async_remote_copy(
            src_ref=src, dst_ref=dst, send_sem=send_sem, recv_sem=recv_sem,
            device_id=device, device_id_type=MESH,
        )

    def greet(device):
        pl.semaphore_signal(barrier, inc=1, device_id=device, device_id_type=MESH)

    barrier = pltpu.get_barrier_semaphore()
    for k in range(1, NY):
        greet(place(y + k, z))
        greet({"dp": (d + k) % NY})
    for k in range(1, NZ):
        greet(place(y, z + k))
    greet({"pipe": (p + 1) % 4})
    greet({"pipe": (p + 3) % 4})
    pl.semaphore_wait(barrier, 2 * (NY - 1) + NZ - 1 + 2)

    wx_self = pltpu.make_async_copy(wo_loc, wx.at[d], lsem.at[0])
    wx_send = [
        remote(wo_loc, wx.at[d], dsend.at[k - 1], drecv.at[k - 1], {"dp": (d + k) % NY})
        for k in range(1, NY)
    ]
    wo_self = pltpu.make_async_copy(wx.at[y], wo.at[y], lsem.at[1])
    wo_send = [
        remote(wx.at[(y + k) % NY], wo.at[y], wsend.at[k - 1], wrecv.at[k - 1], place(y + k, z))
        for k in range(1, NY)
    ]

    def spread_wo():
        wx_self.start()
        for c in wx_send:
            c.start()

    def pass_wo():
        wx_self.wait()
        for c in wx_send:
            c.wait_recv()
        wo_self.start()
        for c in wo_send:
            c.start()

    def wait_wo():
        wo_self.wait()
        for c in wo_send:
            c.wait_recv()

    def turn():
        pl.semaphore_signal(go, inc=1, device_id={"pipe": 1}, device_id_type=MESH)

    def my_turn():
        @pl.when(p == 1)
        def _():
            pl.semaphore_wait(go, 1)

    my_turn()
    spread_wo()
    my_turn()

    @pl.when(p > 0)
    def _():
        pass_wo()

    rows8 = lax.broadcasted_iota(jnp.int32, (8, toks), 0)
    lane = lax.broadcasted_iota(jnp.int32, (8, toks), 1)

    def embed(j):
        act_of = jnp.zeros((8, toks), jnp.int32)
        for fr in range(FRAMES):
            act_of = jnp.where(lane // SPATIAL == fr, acts[plan[j], fr], act_of)
        onehot = (act_of == rows8).astype(jnp.float32)
        return lax.dot_general(
            table[...].astype(jnp.float32), onehot, (((0,), (0,)), ((), ())),
            preferred_element_type=jnp.float32, precision=lax.Precision.HIGHEST,
        )

    embeds = [embed(j) for j in range(2)]
    pipe_copies = [
        remote(out.at[j], hin.at[j], psend.at[j], precv.at[j], {"pipe": (p + 1) % 4})
        for j in range(2)
    ]
    own_f = pl.ds(pl.multiple_of((z * NY + y) * f, f), f)

    def block(j, yy, zz):
        row = ((zz + NZ) % NZ * NY + (yy + NY) % NY) * f
        return xbuf.at[j, pl.ds(pl.multiple_of(row, f), f), :]

    ring = {}

    def ring_send(j, way, dist, k):
        hop = {1: 1, 2: 2, 3: 1, 4: 2}[dist]
        back = dist - hop
        ref = block(j, y - k, z + back if way else z - back)
        c = remote(ref, ref, zsend.at[j, way, dist - 1, k], zrecv.at[j, way, dist - 1, k],
                   place(y, z + NZ - hop if way else z + hop))
        ring[j, way, dist, k] = c
        sends.append(c)
        return c

    ycopies = {}
    for j in range(2):
        for k in range(1, NY):
            ref = block(j, y, z)
            ycopies[j, k] = remote(
                ref, ref, ysend.at[j, k - 1], yrecv.at[j, k - 1], place(y + k, z)
            )
            sends.append(ycopies[j, k])
        for dist in (1, 2):
            for way in range(2):
                ring_send(j, way, dist, 0)

    def cond(j):
        xbuf[j, own_f, :] = (hin[j].astype(jnp.float32) + embeds[j]).astype(jnp.bfloat16)
        for k in (2, 1, 3):
            ycopies[j, k].start()
        for dist in (2, 1):
            for way in range(2):
                ring[j, way, dist, 0].start()
        acc[j] = jnp.zeros_like(acc[j])

    def cond_first(j):
        @pl.when(p == 0)
        def _():
            hin[j] = clips[plan[j]]
            cond(j)

    def cond_later(j):
        @pl.when(p > 0)
        def _():
            pipe_copies[j].wait_recv()
            cond(j)

    square = [jnp.zeros((1, toks), jnp.float32) for _ in range(2)]

    def use(j, zz):
        col = (zz + NZ) % NZ
        x = xbuf[j, pl.ds(pl.multiple_of(col * NY * f, NY * f), NY * f), :]
        acc[j] += jnp.dot(wq[col], x, preferred_element_type=jnp.float32)
        xf = x.astype(jnp.float32)
        square[j] += jnp.sum(xf * xf, axis=0, keepdims=True)

    def xstage(j, i):
        if i == 0:
            for k in (1, 3, 2):
                ycopies[j, k].wait_recv()
                for dist in (2, 1):
                    for way in range(2):
                        ring_send(j, way, dist, k).start()
            use(j, z)
        if i == 1:
            for k in (0, 1, 3, 2):
                for way in range(2):
                    ring[j, way, 2, k].wait_recv()
                    if (k < 2) == (way == 0):
                        ring_send(j, way, 4, k).start()
                    ring_send(j, way, 3, k).start()
            use(j, z - 2)
            use(j, z + 2)
            for k in range(NY):
                for way in range(2):
                    ring[j, way, 1, k].wait_recv()
            use(j, z - 1)
            use(j, z + 1)
        if i == 2:
            for k in range(NY):
                for way in range(2):
                    ring[j, way, 3, k].wait_recv()
            use(j, z - 3)
            use(j, z + 3)
            for k in range(NY):
                ring[j, 0 if k < 2 else 1, 4, k].wait_recv()
            use(j, z + 4)

    kpos = lax.broadcasted_iota(jnp.int32, (toks, toks), 0)
    qpos = lax.broadcasted_iota(jnp.int32, (toks, toks), 1)
    kframe, qframe = kpos // SPATIAL, qpos // SPATIAL
    acopies = {}

    def attention(j):
        same_frame = kframe == qframe
        causal = (kpos % SPATIAL == qpos % SPATIAL) & (kframe <= qframe)
        seen = jnp.zeros((toks, toks), jnp.int32)
        for fr in range(FRAMES):
            seen = jnp.where(kframe == fr, vis[plan[j], fr], seen)
        temporal = jnp.where(causal & ((seen == 1) | same_frame), 1, 0)
        allowed = jnp.where(p % 2 == 0, jnp.where(same_frame, 1, 0), temporal)
        scale = lax.rsqrt(square[j] * (1.0 / (NY * NZ * f)) + 1e-05)
        qkv = (acc[j] * scale).astype(jnp.bfloat16)
        query, keys, values = qkv[:HD], qkv[HD:2 * HD], qkv[2 * HD:]
        scores = lax.dot_general(
            keys, query, (((0,), (0,)), ((), ())), preferred_element_type=jnp.float32
        ) * HD ** (-0.5)
        scores = jnp.where(allowed == 1, scores, -1e30)
        top = jnp.max(scores, axis=0, keepdims=True)
        weights = jnp.exp(scores - top)
        probs = (weights / jnp.sum(weights, axis=0, keepdims=True)).astype(jnp.bfloat16)
        attn = jnp.dot(values, probs, preferred_element_type=jnp.float32)
        own_a = pl.ds(pl.multiple_of(z * HD, HD), HD)
        abuf[j, own_a, :] = attn.astype(jnp.bfloat16)
        for k in (4, 3, 5, 2, 6, 1, 7):
            ref = abuf.at[j, own_a, :]
            c = remote(ref, ref, asend.at[j, k - 1], arecv.at[j, k - 1], place(y, z + k))
            c.start()
            acopies[j, k] = c
            sends.append(c)

    rcopies = {}

    def project(j):
        for k in range(1, NZ):
            acopies[j, k].wait_recv()
        for yy in range(NY):
            part = jnp.dot(wo[yy], abuf[j], preferred_element_type=jnp.float32)
            pacc[j, yy] = part
            pbuf[j, yy] = part.astype(jnp.bfloat16)
        for k in (2, 1, 3):
            c = remote(pbuf.at[j, (y + k) % NY], rbuf.at[j, k - 1],
                       rsend.at[j, k - 1], rrecv.at[j, k - 1], place(y + k, z))
            c.start()
            rcopies[j, k] = c
            sends.append(c)

    def finish(j):
        total = pacc[j, y]
        for k in range(1, NY):
            rcopies[j, k].wait_recv()
            total += rbuf[j, k - 1].astype(jnp.float32)
        out[j] = (xbuf[j, own_f, :].astype(jnp.float32) + total).astype(jnp.bfloat16)

        @pl.when(p < 3)
        def _():
            pipe_copies[j].start()

    cond_first(0)
    cond_later(0)
    xstage(0, 0)
    xstage(0, 1)

    @pl.when(p == 0)
    def _():
        pass_wo()
        turn()

    cond_first(1)
    xstage(0, 2)
    attention(0)
    cond_later(1)
    xstage(1, 0)
    wait_wo()

    @pl.when(p == 0)
    def _():
        turn()

    project(0)
    xstage(1, 1)
    finish(0)
    xstage(1, 2)
    attention(1)
    project(1)
    finish(1)

    for c in sends + wx_send + wo_send:
        c.wait_send()

    @pl.when(p < 3)
    def _():
        for c in pipe_copies:
            c.wait_send()


def shards(
    clips_in, action_ids, frame_visible, plan, qkv_weight, norm_gain, action_table, out_weight
):
    clips, toks, f = clips_in.shape
    n = qkv_weight.shape[2]
    rows = out_weight.shape[1]
    bf16 = jnp.bfloat16
    xt = jnp.swapaxes(clips_in, 1, 2)
    wq = (qkv_weight[0].astype(jnp.float32) * norm_gain[0].astype(jnp.float32)[:, None]).astype(bf16)
    wq = wq.reshape(NY, NZ, f, n).transpose(1, 3, 0, 2).reshape(NZ, n, NY * f)
    wo_loc = out_weight[0].T
    smem = pl.BlockSpec(memory_space=pltpu.SMEM)
    vmem = pl.BlockSpec(memory_space=pltpu.VMEM)
    dma = pltpu.SemaphoreType.DMA
    res = pl.pallas_call(
        kernel,
        out_shape=jax.ShapeDtypeStruct((clips, f, toks), bf16),
        in_specs=[smem] * 3 + [vmem] * 4,
        out_specs=vmem,
        scratch_shapes=[
            pltpu.VMEM((clips, NY * NZ * f, toks), bf16),
            pltpu.VMEM((clips, NZ * HD, toks), bf16),
            pltpu.VMEM((NY, f, rows), bf16),
            pltpu.VMEM((NY, f, rows), bf16),
            pltpu.VMEM((clips, f, toks), bf16),
            pltpu.VMEM((clips, n, toks), jnp.float32),
            pltpu.VMEM((clips, NY, f, toks), jnp.float32),
            pltpu.VMEM((clips, NY, f, toks), bf16),
            pltpu.VMEM((clips, NY - 1, f, toks), bf16),
            dma((2, 3)), dma((2, 3)),
            dma((2, 2, 4, 4)), dma((2, 2, 4, 4)),
            dma((2, 7)), dma((2, 7)),
            dma((2, 3)), dma((2, 3)),
            dma((2,)), dma((2,)),
            dma((3,)), dma((3,)),
            dma((3,)), dma((3,)),
            dma((2,)),
            pltpu.SemaphoreType.REGULAR,
        ],
        compiler_params=pltpu.CompilerParams(
            collective_id=0, has_side_effects=True, vmem_limit_bytes=48 * 1024 * 1024
        ),
    )(plan, action_ids, frame_visible, xt, action_table[0], wq, wo_loc)
    return jnp.swapaxes(res, 1, 2)[None]


def solution(mesh):
    return jax.shard_map(
        shards,
        mesh=mesh,
        in_specs=(
            P("dp", None, "seq"),
            P("dp", None),
            P("dp", None),
            P(),
            P("pipe", None, "seq"),
            P("pipe", None),
            P("pipe", None, "seq"),
            P("pipe", "dp", "seq"),
        ),
        out_specs=P("pipe", "dp", None, "seq"),
        check_vma=False,
    )
```

```python
import jax
import jax.numpy as jnp
from jax import lax
from jax.experimental import pallas as pl
from jax.experimental.pallas import tpu as pltpu
from jax.sharding import PartitionSpec as P

HD = 128
SPATIAL = 16
FRAMES = 8
NY = 4
NZ = 8
MESH = pl.DeviceIdType.MESH


def kernel(
    plan, acts, vis,
    clips, table, gain, w_hbm, wo_loc,
    out,
    w_raw, wq, square, xbuf, abuf, afull, wx, wo, hin, acc, pacc, pbuf, rbuf,
    ysend, yrecv, zsend, zrecv, y2send, y2recv, z2send, z2recv, asend, arecv, rsend, rrecv, psend, precv,
    dsend, drecv, wsend, wrecv, lsem, wsem, go,
):
    p = lax.axis_index("pipe")
    s = lax.axis_index("seq")
    d = lax.axis_index("dp")
    y = s // NZ
    z = s % NZ
    f, toks = hin.shape[1], hin.shape[2]

    def place(yy, zz):
        return {"seq": (yy % NY) * NZ + zz % NZ}

    def remote(src, dst, send_sem, recv_sem, device):
        return pltpu.make_async_remote_copy(
            src_ref=src, dst_ref=dst, send_sem=send_sem, recv_sem=recv_sem,
            device_id=device, device_id_type=MESH,
        )

    def greet(device):
        pl.semaphore_signal(barrier, inc=1, device_id=device, device_id_type=MESH)

    barrier = pltpu.get_barrier_semaphore()
    for k in range(1, NY):
        greet(place(y + k, z))
        greet({"dp": (d + k) % NY})
    for k in range(1, NZ):
        greet(place(y, z + k))
    greet({"pipe": (p + 1) % 4})
    greet({"pipe": (p + 3) % 4})

    w_copy = pltpu.make_async_copy(w_hbm, w_raw, wsem)
    w_copy.start()

    @pl.when(p == 0)
    def _():
        for j in range(2):
            hin[j] = clips[plan[j]]

    w_copy.wait()

    def prepare(col):
        blocks = [
            w_raw[(yy * NZ + col) * f:(yy * NZ + col + 1) * f, :] for yy in range(NY)
        ]
        w = jnp.concatenate(blocks, axis=0).T
        g = [gain[:, (yy * NZ + col) * f:(yy * NZ + col + 1) * f] for yy in range(NY)]
        g = jnp.concatenate(g, axis=1).astype(jnp.float32)
        wq[col] = (w.astype(jnp.float32) * g).astype(jnp.bfloat16)

    for col in range(NZ):
        prepare(col)

    pl.semaphore_wait(barrier, 2 * (NY - 1) + NZ - 1 + 2)

    wx_self = pltpu.make_async_copy(wo_loc, wx.at[d], lsem.at[0])
    wx_send = [
        remote(wo_loc, wx.at[d], dsend.at[k - 1], drecv.at[k - 1], {"dp": (d + k) % NY})
        for k in range(1, NY)
    ]
    wo_self = pltpu.make_async_copy(wx.at[y], wo.at[y], lsem.at[1])
    wo_send = [
        remote(wx.at[(y + k) % NY], wo.at[y], wsend.at[k - 1], wrecv.at[k - 1], place(y + k, z))
        for k in range(1, NY)
    ]

    def wait_wx():
        wx_self.wait()
        for c in wx_send:
            c.wait_recv()

    def wait_wo():
        wo_self.wait()
        for c in wo_send:
            c.wait_recv()

    for c in wx_send:
        c.start()
    wx_self.start()

    @pl.when(p == 1)
    def _():
        pl.semaphore_wait(go, 1)

    @pl.when(p > 0)
    def _():
        wait_wx()
        wo_self.start()
        for c in wo_send:
            c.start()

    rows8 = lax.broadcasted_iota(jnp.int32, (8, toks), 0)
    lane = lax.broadcasted_iota(jnp.int32, (8, toks), 1)

    def embed(j):
        act_of = jnp.zeros((8, toks), jnp.int32)
        for fr in range(FRAMES):
            act_of = jnp.where(lane // SPATIAL == fr, acts[plan[j], fr], act_of)
        onehot = (act_of == rows8).astype(jnp.float32)
        return lax.dot_general(
            table[...].astype(jnp.float32), onehot, (((0,), (0,)), ((), ())),
            preferred_element_type=jnp.float32, precision=lax.Precision.HIGHEST,
        )

    embeds = [embed(j) for j in range(2)]
    pipe_copies = [
        remote(out.at[j], hin.at[j], psend.at[j], precv.at[j], {"pipe": (p + 1) % 4})
        for j in range(2)
    ]
    own_f = pl.ds(pl.multiple_of((z * NY + y) * f, f), f)

    def block(j, yy, zz):
        row = ((zz + NZ) % NZ * NY + (yy + NY) % NY) * f
        return xbuf.at[j, pl.ds(pl.multiple_of(row, f), f), :]

    def block_a(j, yy, zz):
        row = ((yy + NY) % NY * NZ + (zz + NZ) % NZ) * HD
        return afull.at[j, pl.ds(pl.multiple_of(row, HD), HD), :]

    def plan_gather(j, piece, y_send, y_recv, z_send, z_recv):
        first, ring = {}, {}
        for k in range(1, NY):
            ref = piece(j, y, z)
            first[k] = remote(ref, ref, y_send.at[j, k - 1], y_recv.at[j, k - 1], place(y + k, z))
        for k in range(NY):
            for way in range(2):
                for dist in range(1, 5):
                    if dist == 4 and (k < 2) != (way == 0):
                        continue
                    hop = {1: 1, 2: 2, 3: 1, 4: 2}[dist]
                    back = dist - hop
                    ref = piece(j, y - k, z + back if way else z - back)
                    ring[way, dist, k] = remote(
                        ref, ref, z_send.at[j, way, dist - 1, k], z_recv.at[j, way, dist - 1, k],
                        place(y, z + NZ - hop if way else z + hop),
                    )
        return first, ring

    xg = [plan_gather(j, block, ysend, yrecv, zsend, zrecv) for j in range(2)]
    ag = [plan_gather(j, block_a, y2send, y2recv, z2send, z2recv) for j in range(2)]
    acopies, rcopies = {}, {}
    own_a = pl.ds(pl.multiple_of(z * HD, HD), HD)
    for j in range(2):
        for k in range(1, NY):
            rcopies[j, k] = remote(
                pbuf.at[j, (y + k) % NY], rbuf.at[j, k - 1],
                rsend.at[j, k - 1], rrecv.at[j, k - 1], place(y + k, z)
            )
        for k in range(1, NZ):
            ref = abuf.at[j, own_a, :]
            acopies[j, k] = remote(
                ref, ref, asend.at[j, k - 1], arecv.at[j, k - 1], place(y, z + k)
            )

    def launch(gather):
        first, ring = gather
        for k in (2, 1, 3):
            first[k].start()
        for dist in (2, 1):
            for way in range(2):
                ring[way, dist, 0].start()

    def stage(gather, i, use=None):
        first, ring = gather
        if i == 0:
            for k in (1, 3, 2):
                first[k].wait_recv()
                for dist in (2, 1):
                    for way in range(2):
                        ring[way, dist, k].start()
            if use:
                use(z)
        if i == 1:
            for k in (0, 1, 3, 2):
                for way in range(2):
                    ring[way, 2, k].wait_recv()
                    if (k < 2) == (way == 0):
                        ring[way, 4, k].start()
                    ring[way, 3, k].start()
            if use:
                use(z - 2)
                use(z + 2)
            for k in range(NY):
                for way in range(2):
                    ring[way, 1, k].wait_recv()
            if use:
                use(z - 1)
                use(z + 1)
        if i == 2:
            for k in range(NY):
                for way in range(2):
                    ring[way, 3, k].wait_recv()
            if use:
                use(z - 3)
                use(z + 3)
            for k in range(NY):
                ring[0 if k < 2 else 1, 4, k].wait_recv()
            if use:
                use(z + 4)

    def cond(j):
        xbuf[j, own_f, :] = (hin[j].astype(jnp.float32) + embeds[j]).astype(jnp.bfloat16)
        launch(xg[j])
        acc[j] = jnp.zeros_like(acc[j])
        square[j] = jnp.zeros_like(square[j])

    def arrive(j):
        pipe_copies[j].wait_recv()

    def use(j, zz):
        col = (zz + NZ) % NZ
        x = xbuf[j, pl.ds(pl.multiple_of(col * NY * f, NY * f), NY * f), :]
        acc[j] += jnp.dot(wq[col], x, preferred_element_type=jnp.float32)
        xf = x.astype(jnp.float32)
        square[j] += jnp.sum(xf * xf, axis=0, keepdims=True)

    def xstage(j, i):
        stage(xg[j], i, lambda zz: use(j, zz))

    kpos = lax.broadcasted_iota(jnp.int32, (toks, toks), 0)
    qpos = lax.broadcasted_iota(jnp.int32, (toks, toks), 1)
    kframe, qframe = kpos // SPATIAL, qpos // SPATIAL

    def attention(j, whole=False):
        same_frame = kframe == qframe
        causal = (kpos % SPATIAL == qpos % SPATIAL) & (kframe <= qframe)
        seen = jnp.zeros((toks, toks), jnp.int32)
        for fr in range(FRAMES):
            seen = jnp.where(kframe == fr, vis[plan[j], fr], seen)
        temporal = jnp.where(causal & ((seen == 1) | same_frame), 1, 0)
        allowed = jnp.where(p % 2 == 0, jnp.where(same_frame, 1, 0), temporal)
        scale = lax.rsqrt(square[j] * (1.0 / (NY * NZ * f)) + 1e-05)
        qkv = (acc[j] * scale).astype(jnp.bfloat16)
        query, keys, values = qkv[:HD], qkv[HD:2 * HD], qkv[2 * HD:]
        scores = lax.dot_general(
            keys, query, (((0,), (0,)), ((), ())), preferred_element_type=jnp.float32
        ) * HD ** (-0.5)
        scores = jnp.where(allowed == 1, scores, -1e30)
        top = jnp.max(scores, axis=0, keepdims=True)
        weights = jnp.exp(scores - top)
        probs = (weights / jnp.sum(weights, axis=0, keepdims=True)).astype(jnp.bfloat16)
        attn = jnp.dot(values, probs, preferred_element_type=jnp.float32)
        if whole:
            own = pl.ds(pl.multiple_of((y * NZ + z) * HD, HD), HD)
            afull[j, own, :] = attn.astype(jnp.bfloat16)
            launch(ag[j])
            return
        abuf[j, own_a, :] = attn.astype(jnp.bfloat16)
        for k in (4, 3, 5, 2, 6, 1, 7):
            acopies[j, k].start()

    def project(j):
        for k in range(1, NZ):
            acopies[j, k].wait_recv()
        for yy in range(NY):
            part = jnp.dot(wo[yy], abuf[j], preferred_element_type=jnp.float32)
            pacc[j, yy] = part
            pbuf[j, yy] = part.astype(jnp.bfloat16)
        for k in (2, 1, 3):
            rcopies[j, k].start()

    def finish_whole(j):
        total = xbuf[j, own_f, :].astype(jnp.float32)
        for yy in range(NY):
            total += jnp.dot(
                wx[yy], afull[j, yy * NZ * HD:(yy + 1) * NZ * HD, :],
                preferred_element_type=jnp.float32,
            )
        out[j] = total.astype(jnp.bfloat16)
        pipe_copies[j].start()

    def finish(j):
        total = pacc[j, y]
        for k in range(1, NY):
            rcopies[j, k].wait_recv()
            total += rbuf[j, k - 1].astype(jnp.float32)
        out[j] = (xbuf[j, own_f, :].astype(jnp.float32) + total).astype(jnp.bfloat16)

        @pl.when(p < 3)
        def _():
            pipe_copies[j].start()

    @pl.when(p == 0)
    def _():
        cond(0)
        xstage(0, 0)
        xstage(0, 1)
        cond(1)
        xstage(0, 2)
        attention(0, whole=True)
        xstage(1, 0)
        stage(ag[0], 0)
        pl.semaphore_signal(go, inc=1, device_id={"pipe": 1}, device_id_type=MESH)
        xstage(1, 1)
        stage(ag[0], 1)
        xstage(1, 2)
        attention(1, whole=True)
        wait_wx()
        stage(ag[0], 2)
        finish_whole(0)
        stage(ag[1], 0)
        stage(ag[1], 1)
        stage(ag[1], 2)
        finish_whole(1)
        for first, ring in ag:
            for c in list(first.values()) + list(ring.values()):
                c.wait_send()

    @pl.when(p > 0)
    def _():
        arrive(0)
        cond(0)
        xstage(0, 0)
        xstage(0, 1)
        xstage(0, 2)
        attention(0)
        arrive(1)
        cond(1)
        xstage(1, 0)
        wait_wo()
        project(0)
        xstage(1, 1)
        finish(0)
        xstage(1, 2)
        attention(1)
        project(1)
        finish(1)
        for c in list(acopies.values()) + list(rcopies.values()) + wo_send:
            c.wait_send()

    for first, ring in xg:
        for c in list(first.values()) + list(ring.values()):
            c.wait_send()
    for c in wx_send:
        c.wait_send()

    @pl.when(p < 3)
    def _():
        for c in pipe_copies:
            c.wait_send()


def shards(
    clips_in, action_ids, frame_visible, plan, qkv_weight, norm_gain, action_table, out_weight
):
    clips, toks, f = clips_in.shape
    n = qkv_weight.shape[2]
    rows = out_weight.shape[1]
    bf16 = jnp.bfloat16
    xt = jnp.swapaxes(clips_in, 1, 2)
    smem = pl.BlockSpec(memory_space=pltpu.SMEM)
    vmem = pl.BlockSpec(memory_space=pltpu.VMEM)
    dma = pltpu.SemaphoreType.DMA
    res = pl.pallas_call(
        kernel,
        out_shape=jax.ShapeDtypeStruct((clips, f, toks), bf16),
        in_specs=[smem] * 3 + [vmem] * 3 + [pl.BlockSpec(memory_space=pl.ANY), vmem],
        out_specs=vmem,
        scratch_shapes=[
            pltpu.VMEM((NY * NZ * f, n), bf16),
            pltpu.VMEM((NZ, n, NY * f), bf16),
            pltpu.VMEM((clips, 1, toks), jnp.float32),
            pltpu.VMEM((clips, NY * NZ * f, toks), bf16),
            pltpu.VMEM((clips, NZ * HD, toks), bf16),
            pltpu.VMEM((clips, NY * NZ * HD, toks), bf16),
            pltpu.VMEM((NY, f, rows), bf16),
            pltpu.VMEM((NY, f, rows), bf16),
            pltpu.VMEM((clips, f, toks), bf16),
            pltpu.VMEM((clips, n, toks), jnp.float32),
            pltpu.VMEM((clips, NY, f, toks), jnp.float32),
            pltpu.VMEM((clips, NY, f, toks), bf16),
            pltpu.VMEM((clips, NY - 1, f, toks), bf16),
            dma((2, 3)), dma((2, 3)),
            dma((2, 2, 4, 4)), dma((2, 2, 4, 4)),
            dma((2, 3)), dma((2, 3)),
            dma((2, 2, 4, 4)), dma((2, 2, 4, 4)),
            dma((2, 7)), dma((2, 7)),
            dma((2, 3)), dma((2, 3)),
            dma((2,)), dma((2,)),
            dma((3,)), dma((3,)),
            dma((3,)), dma((3,)),
            dma((2,)), dma,
            pltpu.SemaphoreType.REGULAR,
        ],
        compiler_params=pltpu.CompilerParams(
            collective_id=0, has_side_effects=True, vmem_limit_bytes=63 * 1024 * 1024
        ),
    )(plan, action_ids, frame_visible, xt, action_table[0], norm_gain, qkv_weight[0], out_weight[0].T)
    return jnp.swapaxes(res, 1, 2)[None]


def solution(mesh):
    return jax.shard_map(
        shards,
        mesh=mesh,
        in_specs=(
            P("dp", None, "seq"),
            P("dp", None),
            P("dp", None),
            P(),
            P("pipe", None, "seq"),
            P("pipe", None),
            P("pipe", None, "seq"),
            P("pipe", "dp", "seq"),
        ),
        out_specs=P("pipe", "dp", None, "seq"),
        check_vma=False,
    )
```

```python
import jax
import jax.numpy as jnp
from jax import lax
from jax.experimental import pallas as pl
from jax.experimental.pallas import tpu as pltpu
from jax.sharding import PartitionSpec as P

HD = 128
SPATIAL = 16
FRAMES = 8
NY = 4
NZ = 8
MESH = pl.DeviceIdType.MESH


def kernel(
    plan_in, acts_in, vis_in, clips_in, table_in, gain_in, w_in, wo_in,
    out,
    plan, acts, vis, clips, table, gain, wo_loc, w_raw, wq, embeds, square, xbuf, abuf, afull, wx, wo, hin, acc, pacc, pbuf, rbuf,
    ysend, yrecv, zsend, zrecv, y2send, y2recv, z2send, z2recv, asend, arecv, rsend, rrecv, psend, precv,
    dsend, drecv, wsend, wrecv, lsem, wsem, go,
):
    p = lax.axis_index("pipe")
    s = lax.axis_index("seq")
    d = lax.axis_index("dp")
    y = s // NZ
    z = s % NZ
    f, toks = hin.shape[1], hin.shape[2]

    def place(yy, zz):
        return {"seq": (yy % NY) * NZ + zz % NZ}

    def remote(src, dst, send_sem, recv_sem, device):
        return pltpu.make_async_remote_copy(
            src_ref=src, dst_ref=dst, send_sem=send_sem, recv_sem=recv_sem,
            device_id=device, device_id_type=MESH,
        )

    def greet(device):
        pl.semaphore_signal(barrier, inc=1, device_id=device, device_id_type=MESH)

    barrier = pltpu.get_barrier_semaphore()
    for k in range(1, NY):
        greet(place(y + k, z))
        greet({"dp": (d + k) % NY})
    for k in range(1, NZ):
        greet(place(y, z + k))
    greet({"pipe": (p + 1) % 4})
    greet({"pipe": (p + 3) % 4})

    loads = [
        pltpu.make_async_copy(src, dst, wsem.at[i])
        for i, (src, dst) in enumerate((
            (plan_in, plan), (acts_in, acts), (clips_in, clips), (table_in, table),
            (vis_in, vis), (gain_in, gain), (w_in, w_raw), (wo_in, wo_loc),
        ))
    ]
    for c in loads:
        c.start()

    rows8 = lax.broadcasted_iota(jnp.int32, (8, toks), 0)
    lane = lax.broadcasted_iota(jnp.int32, (8, toks), 1)

    def embed(j):
        act_of = jnp.zeros((8, toks), jnp.int32)
        for fr in range(FRAMES):
            act_of = jnp.where(lane // SPATIAL == fr, acts[plan[j], fr], act_of)
        onehot = (act_of == rows8).astype(jnp.float32)
        return lax.dot_general(
            table[...].astype(jnp.float32), onehot, (((0,), (0,)), ((), ())),
            preferred_element_type=jnp.float32, precision=lax.Precision.HIGHEST,
        )

    for c in loads[:4]:
        c.wait()
    for j in range(2):
        embeds[j] = embed(j)
    own_f = pl.ds(pl.multiple_of((z * NY + y) * f, f), f)

    def condition(j, stream):
        xbuf[j, own_f, :] = (stream.astype(jnp.float32) + embeds[j]).astype(jnp.bfloat16)

    @pl.when(p == 0)
    def _():
        for j in range(2):
            condition(j, clips[plan[j]])

    for c in loads[4:7]:
        c.wait()

    def prepare(col):
        blocks = [
            w_raw[(yy * NZ + col) * f:(yy * NZ + col + 1) * f, :] for yy in range(NY)
        ]
        w = jnp.concatenate(blocks, axis=0).T
        g = [gain[:, (yy * NZ + col) * f:(yy * NZ + col + 1) * f] for yy in range(NY)]
        g = jnp.concatenate(g, axis=1).astype(jnp.float32)
        wq[col] = (w.astype(jnp.float32) * g).astype(jnp.bfloat16)

    for col in range(NZ):
        prepare(col)

    pl.semaphore_wait(barrier, 2 * (NY - 1) + NZ - 1 + 2)

    wx_self = pltpu.make_async_copy(wo_loc, wx.at[d], lsem.at[0])
    wx_send = [
        remote(wo_loc, wx.at[d], dsend.at[k - 1], drecv.at[k - 1], {"dp": (d + k) % NY})
        for k in range(1, NY)
    ]
    wo_self = pltpu.make_async_copy(wx.at[y], wo.at[y], lsem.at[1])
    wo_send = [
        remote(wx.at[(y + k) % NY], wo.at[y], wsend.at[k - 1], wrecv.at[k - 1], place(y + k, z))
        for k in range(1, NY)
    ]

    def wait_wx():
        wx_self.wait()
        for c in wx_send:
            c.wait_recv()

    def wait_wo():
        wo_self.wait()
        for c in wo_send:
            c.wait_recv()

    pipe_copies = [
        remote(out.at[j], hin.at[j], psend.at[j], precv.at[j], {"pipe": (p + 1) % 4})
        for j in range(2)
    ]
    def block(j, yy, zz):
        row = ((zz + NZ) % NZ * NY + (yy + NY) % NY) * f
        return xbuf.at[j, pl.ds(pl.multiple_of(row, f), f), :]

    def block_a(j, yy, zz):
        row = ((yy + NY) % NY * NZ + (zz + NZ) % NZ) * HD
        return afull.at[j, pl.ds(pl.multiple_of(row, HD), HD), :]

    def plan_gather(j, piece, y_send, y_recv, z_send, z_recv):
        first, ring = {}, {}
        for k in range(1, NY):
            ref = piece(j, y, z)
            first[k] = remote(ref, ref, y_send.at[j, k - 1], y_recv.at[j, k - 1], place(y + k, z))
        for k in range(NY):
            for way in range(2):
                for dist in range(1, 5):
                    if dist == 4 and (k < 2) != (way == 0):
                        continue
                    hop = {1: 1, 2: 2, 3: 1, 4: 2}[dist]
                    back = dist - hop
                    ref = piece(j, y - k, z + back if way else z - back)
                    ring[way, dist, k] = remote(
                        ref, ref, z_send.at[j, way, dist - 1, k], z_recv.at[j, way, dist - 1, k],
                        place(y, z + NZ - hop if way else z + hop),
                    )
        return first, ring

    xg = [plan_gather(j, block, ysend, yrecv, zsend, zrecv) for j in range(2)]
    ag = [plan_gather(j, block_a, y2send, y2recv, z2send, z2recv) for j in range(2)]
    acopies, rcopies = {}, {}
    own_a = pl.ds(pl.multiple_of(z * HD, HD), HD)
    for j in range(2):
        for k in range(1, NY):
            rcopies[j, k] = remote(
                pbuf.at[j, (y + k) % NY], rbuf.at[j, k - 1],
                rsend.at[j, k - 1], rrecv.at[j, k - 1], place(y + k, z)
            )
        for k in range(1, NZ):
            ref = abuf.at[j, own_a, :]
            acopies[j, k] = remote(
                ref, ref, asend.at[j, k - 1], arecv.at[j, k - 1], place(y, z + k)
            )

    def launch(gather):
        first, ring = gather
        for k in (2, 1, 3):
            first[k].start()
        for dist in (2, 1):
            for way in range(2):
                ring[way, dist, 0].start()

    def stage(gather, i, use=None):
        first, ring = gather
        if i == 0:
            for k in (1, 3, 2):
                first[k].wait_recv()
                for way in range(2):
                    ring[way, 2, k].start()
            for k in range(1, NY):
                for way in range(2):
                    ring[way, 1, k].start()
            if use:
                use(z)
        if i == 1:
            for k in (0, 1, 3, 2):
                for way in range(2):
                    ring[way, 2, k].wait_recv()
                    if (k < 2) == (way == 0):
                        ring[way, 4, k].start()
                    ring[way, 3, k].start()
            if use:
                use(z - 2)
                use(z + 2)
            for k in range(NY):
                for way in range(2):
                    ring[way, 1, k].wait_recv()
            if use:
                use(z - 1)
                use(z + 1)
        if i == 2:
            for k in range(NY):
                for way in range(2):
                    ring[way, 3, k].wait_recv()
            if use:
                use(z - 3)
                use(z + 3)
            for k in range(NY):
                ring[0 if k < 2 else 1, 4, k].wait_recv()
            if use:
                use(z + 4)

    def cond(j):
        condition(j, hin[j])
        launch(xg[j])

    for j in range(2):
        acc[j] = jnp.zeros_like(acc[j])
        square[j] = jnp.zeros_like(square[j])

    def arrive(j):
        pipe_copies[j].wait_recv()

    @pl.when(p == 0)
    def _():
        launch(xg[0])

    loads[7].wait()
    for c in wx_send:
        c.start()
    wx_self.start()

    @pl.when(p == 1)
    def _():
        pl.semaphore_wait(go, 1)

    @pl.when(p > 0)
    def _():
        wait_wx()
        wo_self.start()
        for c in wo_send:
            c.start()

    def use(j, zz):
        col = (zz + NZ) % NZ
        x = xbuf[j, pl.ds(pl.multiple_of(col * NY * f, NY * f), NY * f), :]
        acc[j] += jnp.dot(wq[col], x, preferred_element_type=jnp.float32)
        xf = x.astype(jnp.float32)
        square[j] += jnp.sum(xf * xf, axis=0, keepdims=True)

    def xstage(j, i):
        stage(xg[j], i, lambda zz: use(j, zz))

    kpos = lax.broadcasted_iota(jnp.int32, (toks, toks), 0)
    qpos = lax.broadcasted_iota(jnp.int32, (toks, toks), 1)
    kframe, qframe = kpos // SPATIAL, qpos // SPATIAL

    def attention(j, whole=False):
        same_frame = kframe == qframe
        causal = (kpos % SPATIAL == qpos % SPATIAL) & (kframe <= qframe)
        seen = jnp.zeros((toks, toks), jnp.int32)
        for fr in range(FRAMES):
            seen = jnp.where(kframe == fr, vis[plan[j], fr], seen)
        temporal = jnp.where(causal & ((seen == 1) | same_frame), 1, 0)
        allowed = jnp.where(p % 2 == 0, jnp.where(same_frame, 1, 0), temporal)
        scale = lax.rsqrt(square[j] * (1.0 / (NY * NZ * f)) + 1e-05)
        qkv = (acc[j] * scale).astype(jnp.bfloat16)
        query, keys, values = qkv[:HD], qkv[HD:2 * HD], qkv[2 * HD:]
        scores = lax.dot_general(
            keys, query, (((0,), (0,)), ((), ())), preferred_element_type=jnp.float32
        ) * HD ** (-0.5)
        scores = jnp.where(allowed == 1, scores, -1e30)
        top = jnp.max(scores, axis=0, keepdims=True)
        weights = jnp.exp(scores - top)
        probs = (weights / jnp.sum(weights, axis=0, keepdims=True)).astype(jnp.bfloat16)
        attn = jnp.dot(values, probs, preferred_element_type=jnp.float32)
        if whole:
            own = pl.ds(pl.multiple_of((y * NZ + z) * HD, HD), HD)
            afull[j, own, :] = attn.astype(jnp.bfloat16)
            launch(ag[j])
            return
        abuf[j, own_a, :] = attn.astype(jnp.bfloat16)
        for k in (4, 3, 5, 2, 6, 1, 7):
            acopies[j, k].start()

    def project(j):
        for k in range(1, NZ):
            acopies[j, k].wait_recv()
        for yy in range(NY):
            part = jnp.dot(wo[yy], abuf[j], preferred_element_type=jnp.float32)
            pacc[j, yy] = part
            pbuf[j, yy] = part.astype(jnp.bfloat16)
        for k in (2, 1, 3):
            rcopies[j, k].start()

    def finish_whole(j):
        total = xbuf[j, own_f, :].astype(jnp.float32)
        for yy in range(NY):
            total += jnp.dot(
                wx[yy], afull[j, yy * NZ * HD:(yy + 1) * NZ * HD, :],
                preferred_element_type=jnp.float32,
            )
        out[j] = total.astype(jnp.bfloat16)
        pipe_copies[j].start()

    def finish(j):
        total = pacc[j, y]
        for k in range(1, NY):
            rcopies[j, k].wait_recv()
            total += rbuf[j, k - 1].astype(jnp.float32)
        out[j] = (xbuf[j, own_f, :].astype(jnp.float32) + total).astype(jnp.bfloat16)

        @pl.when(p < 3)
        def _():
            pipe_copies[j].start()

    @pl.when(p == 0)
    def _():
        xstage(0, 0)
        xstage(0, 1)
        launch(xg[1])
        xstage(0, 2)
        attention(0, whole=True)
        xstage(1, 0)
        stage(ag[0], 0)
        pl.semaphore_signal(go, inc=1, device_id={"pipe": 1}, device_id_type=MESH)
        xstage(1, 1)
        stage(ag[0], 1)
        xstage(1, 2)
        attention(1, whole=True)
        wait_wx()
        stage(ag[0], 2)
        finish_whole(0)
        stage(ag[1], 0)
        stage(ag[1], 1)
        stage(ag[1], 2)
        finish_whole(1)
        for first, ring in ag:
            for c in list(first.values()) + list(ring.values()):
                c.wait_send()

    @pl.when(p > 0)
    def _():
        arrive(0)
        cond(0)
        xstage(0, 0)
        xstage(0, 1)
        arrive(1)
        cond(1)
        xstage(0, 2)
        attention(0)
        xstage(1, 0)
        wait_wo()
        project(0)
        xstage(1, 1)
        finish(0)
        xstage(1, 2)
        attention(1)
        project(1)
        finish(1)
        for c in list(acopies.values()) + list(rcopies.values()) + wo_send:
            c.wait_send()

    for first, ring in xg:
        for c in list(first.values()) + list(ring.values()):
            c.wait_send()
    for c in wx_send:
        c.wait_send()

    @pl.when(p < 3)
    def _():
        for c in pipe_copies:
            c.wait_send()


def shards(
    clips_in, action_ids, frame_visible, plan, qkv_weight, norm_gain, action_table, out_weight
):
    clips, toks, f = clips_in.shape
    n = qkv_weight.shape[2]
    rows = out_weight.shape[1]
    bf16 = jnp.bfloat16
    xt = jnp.swapaxes(clips_in, 1, 2)
    vmem = pl.BlockSpec(memory_space=pltpu.VMEM)
    dma = pltpu.SemaphoreType.DMA
    res = pl.pallas_call(
        kernel,
        out_shape=jax.ShapeDtypeStruct((clips, f, toks), bf16),
        in_specs=[pl.BlockSpec(memory_space=pl.ANY)] * 8,
        out_specs=vmem,
        scratch_shapes=[
            pltpu.SMEM(plan.shape, jnp.int32),
            pltpu.SMEM(action_ids.shape, jnp.int32),
            pltpu.SMEM(frame_visible.shape, jnp.int32),
            pltpu.VMEM((clips, f, toks), bf16),
            pltpu.VMEM(action_table.shape[1:], bf16),
            pltpu.VMEM(norm_gain.shape, bf16),
            pltpu.VMEM((f, rows), bf16),
            pltpu.VMEM((NY * NZ * f, n), bf16),
            pltpu.VMEM((NZ, n, NY * f), bf16),
            pltpu.VMEM((clips, f, toks), jnp.float32),
            pltpu.VMEM((clips, 1, toks), jnp.float32),
            pltpu.VMEM((clips, NY * NZ * f, toks), bf16),
            pltpu.VMEM((clips, NZ * HD, toks), bf16),
            pltpu.VMEM((clips, NY * NZ * HD, toks), bf16),
            pltpu.VMEM((NY, f, rows), bf16),
            pltpu.VMEM((NY, f, rows), bf16),
            pltpu.VMEM((clips, f, toks), bf16),
            pltpu.VMEM((clips, n, toks), jnp.float32),
            pltpu.VMEM((clips, NY, f, toks), jnp.float32),
            pltpu.VMEM((clips, NY, f, toks), bf16),
            pltpu.VMEM((clips, NY - 1, f, toks), bf16),
            dma((2, 3)), dma((2, 3)),
            dma((2, 2, 4, 4)), dma((2, 2, 4, 4)),
            dma((2, 3)), dma((2, 3)),
            dma((2, 2, 4, 4)), dma((2, 2, 4, 4)),
            dma((2, 7)), dma((2, 7)),
            dma((2, 3)), dma((2, 3)),
            dma((2,)), dma((2,)),
            dma((3,)), dma((3,)),
            dma((3,)), dma((3,)),
            dma((2,)), dma((8,)),
            pltpu.SemaphoreType.REGULAR,
        ],
        compiler_params=pltpu.CompilerParams(
            collective_id=0, has_side_effects=True, vmem_limit_bytes=63 * 1024 * 1024
        ),
    )(plan, action_ids, frame_visible, xt, action_table[0], norm_gain, qkv_weight[0], out_weight[0].T)
    return jnp.swapaxes(res, 1, 2)[None]


def solution(mesh):
    return jax.shard_map(
        shards,
        mesh=mesh,
        in_specs=(
            P("dp", None, "seq"),
            P("dp", None),
            P("dp", None),
            P(),
            P("pipe", None, "seq"),
            P("pipe", None),
            P("pipe", None, "seq"),
            P("pipe", "dp", "seq"),
        ),
        out_specs=P("pipe", "dp", None, "seq"),
        check_vma=False,
    )
```

```python
import jax
import jax.numpy as jnp
from jax import lax
from jax.experimental import pallas as pl
from jax.experimental.pallas import tpu as pltpu
from jax.sharding import PartitionSpec as P

HD = 128
SPATIAL = 16
FRAMES = 8
NY = 4
NZ = 8
MESH = pl.DeviceIdType.MESH


def kernel(
    plan_in, acts_in, vis_in, clips_in, table_in, gain_in, w_in, wo_in,
    out,
    plan, acts, vis, clips, table, gain, wo_loc, w_raw, wq, embeds, square, xbuf, abuf, afull, wx, wo, hin, cbuf, hback, acc, pacc, pbuf, rbuf,
    ysend, yrecv, zsend, zrecv, y2send, y2recv, z2send, z2recv, asend, arecv, rsend, rrecv, psend, precv, csend, crecv, bsend, brecv,
    dsend, drecv, wsend, wrecv, lsem, wsem, go,
):
    p = lax.axis_index("pipe")
    s = lax.axis_index("seq")
    d = lax.axis_index("dp")
    y = s // NZ
    z = s % NZ
    f, toks = hin.shape[1], hin.shape[2]

    def place(yy, zz):
        return {"seq": (yy % NY) * NZ + zz % NZ}

    def remote(src, dst, send_sem, recv_sem, device):
        return pltpu.make_async_remote_copy(
            src_ref=src, dst_ref=dst, send_sem=send_sem, recv_sem=recv_sem,
            device_id=device, device_id_type=MESH,
        )

    def greet(device):
        pl.semaphore_signal(barrier, inc=1, device_id=device, device_id_type=MESH)

    barrier = pltpu.get_barrier_semaphore()
    for k in range(1, NY):
        greet(place(y + k, z))
        greet({"dp": (d + k) % NY})
    for k in range(1, NZ):
        greet(place(y, z + k))
    greet({"pipe": (p + 1) % 4})
    greet({"pipe": (p + 3) % 4})
    hands_on = (p + 1) // 2 % 2

    @pl.when(p >= 2)
    def _():
        for k in range(1, NY):
            greet({"pipe": p - 1, "seq": (y + k) % NY * NZ + z})

    loads = [
        pltpu.make_async_copy(src, dst, wsem.at[i])
        for i, (src, dst) in enumerate((
            (plan_in, plan), (acts_in, acts), (clips_in, clips), (table_in, table),
            (vis_in, vis), (gain_in, gain), (w_in, w_raw), (wo_in, wo_loc),
        ))
    ]
    for c in loads:
        c.start()

    rows8 = lax.broadcasted_iota(jnp.int32, (8, toks), 0)
    lane = lax.broadcasted_iota(jnp.int32, (8, toks), 1)

    def embed(j):
        act_of = jnp.zeros((8, toks), jnp.int32)
        for fr in range(FRAMES):
            act_of = jnp.where(lane // SPATIAL == fr, acts[plan[j], fr], act_of)
        onehot = (act_of == rows8).astype(jnp.float32)
        return lax.dot_general(
            table[...].astype(jnp.float32), onehot, (((0,), (0,)), ((), ())),
            preferred_element_type=jnp.float32, precision=lax.Precision.HIGHEST,
        )

    for c in loads[:4]:
        c.wait()
    for j in range(2):
        embeds[j] = embed(j)
    own_f = pl.ds(pl.multiple_of((z * NY + y) * f, f), f)

    def condition(j, stream):
        xbuf[j, own_f, :] = (stream.astype(jnp.float32) + embeds[j]).astype(jnp.bfloat16)

    @pl.when(p == 0)
    def _():
        for j in range(2):
            condition(j, clips[plan[j]])

    for c in loads[4:7]:
        c.wait()

    def prepare(col):
        blocks = [
            w_raw[(yy * NZ + col) * f:(yy * NZ + col + 1) * f, :] for yy in range(NY)
        ]
        w = jnp.concatenate(blocks, axis=0).T
        g = [gain[:, (yy * NZ + col) * f:(yy * NZ + col + 1) * f] for yy in range(NY)]
        g = jnp.concatenate(g, axis=1).astype(jnp.float32)
        wq[col] = (w.astype(jnp.float32) * g).astype(jnp.bfloat16)

    for col in range(NZ):
        prepare(col)

    pl.semaphore_wait(barrier, 2 * (NY - 1) + NZ - 1 + 2 + (NY - 1) * hands_on)

    wx_self = pltpu.make_async_copy(wo_loc, wx.at[d], lsem.at[0])
    wx_send = [
        remote(wo_loc, wx.at[d], dsend.at[k - 1], drecv.at[k - 1], {"dp": (d + k) % NY})
        for k in range(1, NY)
    ]
    wo_self = pltpu.make_async_copy(wx.at[y], wo.at[y], lsem.at[1])
    wo_send = [
        remote(wx.at[(y + k) % NY], wo.at[y], wsend.at[k - 1], wrecv.at[k - 1], place(y + k, z))
        for k in range(1, NY)
    ]

    def wait_wx():
        wx_self.wait()
        for c in wx_send:
            c.wait_recv()

    def wait_wo():
        wo_self.wait()
        for c in wo_send:
            c.wait_recv()

    pipe_copies = [
        remote(out.at[j], hin.at[j], psend.at[j], precv.at[j], {"pipe": (p + 1) % 4})
        for j in range(2)
    ]
    def block(j, yy, zz):
        row = ((zz + NZ) % NZ * NY + (yy + NY) % NY) * f
        return xbuf.at[j, pl.ds(pl.multiple_of(row, f), f), :]

    def block_a(j, yy, zz):
        row = ((yy + NY) % NY * NZ + (zz + NZ) % NZ) * HD
        return afull.at[j, pl.ds(pl.multiple_of(row, HD), HD), :]

    def plan_gather(j, piece, y_send, y_recv, z_send, z_recv):
        first, ring = {}, {}
        for k in range(1, NY):
            ref = piece(j, y, z)
            first[k] = remote(ref, ref, y_send.at[j, k - 1], y_recv.at[j, k - 1], place(y + k, z))
        for k in range(NY):
            for way in range(2):
                for dist in range(1, 5):
                    if dist == 4 and (k < 2) != (way == 0):
                        continue
                    hop = {1: 1, 2: 2, 3: 1, 4: 2}[dist]
                    back = dist - hop
                    ref = piece(j, y - k, z + back if way else z - back)
                    ring[way, dist, k] = remote(
                        ref, ref, z_send.at[j, way, dist - 1, k], z_recv.at[j, way, dist - 1, k],
                        place(y, z + NZ - hop if way else z + hop),
                    )
        return first, ring

    xg = [plan_gather(j, block, ysend, yrecv, zsend, zrecv) for j in range(2)]
    ag = [plan_gather(j, block_a, y2send, y2recv, z2send, z2recv) for j in range(2)]
    acopies, rcopies = {}, {}
    onward = [
        remote(xbuf.at[j, own_f, :], cbuf.at[j], csend.at[j], crecv.at[j], {"pipe": (p + 1) % 4})
        for j in range(2)
    ]
    backward = [
        remote(hin.at[j], hback.at[j], bsend.at[j], brecv.at[j], {"pipe": (p + 3) % 4})
        for j in range(2)
    ]
    own_a = pl.ds(pl.multiple_of(z * HD, HD), HD)
    for j in range(2):
        for k in range(NY):
            rcopies[j, k] = remote(
                pbuf.at[j, (y + k) % NY], rbuf.at[j, p // 3, k],
                rsend.at[j, k], rrecv.at[j, p // 3, k],
                {"pipe": p + 1 - p // 3, "seq": (y + k) % NY * NZ + z},
            )
        for k in range(1, NZ):
            ref = abuf.at[j, own_a, :]
            acopies[j, k] = remote(
                ref, ref, asend.at[j, k - 1], arecv.at[j, k - 1], place(y, z + k)
            )

    def launch(gather):
        first, ring = gather
        for k in (2, 1, 3):
            first[k].start()
        for dist in (2, 1):
            for way in range(2):
                ring[way, dist, 0].start()

    def stage(gather, i, use=None):
        first, ring = gather
        if i == 0:
            for k in (1, 3, 2):
                first[k].wait_recv()
                for way in range(2):
                    ring[way, 2, k].start()
            for k in range(1, NY):
                for way in range(2):
                    ring[way, 1, k].start()
            if use:
                use(z)
        if i == 1:
            for k in (0, 1, 3, 2):
                for way in range(2):
                    ring[way, 2, k].wait_recv()
                    if (k < 2) == (way == 0):
                        ring[way, 4, k].start()
                    ring[way, 3, k].start()
            if use:
                use(z - 2)
                use(z + 2)
            for k in range(NY):
                for way in range(2):
                    ring[way, 1, k].wait_recv()
            if use:
                use(z - 1)
                use(z + 1)
        if i == 2:
            for k in range(NY):
                for way in range(2):
                    ring[way, 3, k].wait_recv()
            if use:
                use(z - 3)
                use(z + 3)
            for k in range(NY):
                ring[0 if k < 2 else 1, 4, k].wait_recv()
            if use:
                use(z + 4)

    def cond(j):
        condition(j, hin[j])
        launch(xg[j])

        @pl.when(hands_on == 1)
        def _():
            onward[j].start()

    for j in range(2):
        acc[j] = jnp.zeros_like(acc[j])
        square[j] = jnp.zeros_like(square[j])

    def collect(j, g, k):
        pltpu.make_async_copy(pbuf.at[j, 0], rbuf.at[j, g, k], rrecv.at[j, g, k]).wait()
        return rbuf[j, g, k].astype(jnp.float32)

    def arrive(j):
        @pl.when(p == 1)
        def _():
            pipe_copies[j].wait_recv()

        @pl.when(p >= 2)
        def _():
            onward[j].wait_recv()
            total = cbuf[j].astype(jnp.float32)
            for k in range(NY):
                total += collect(j, 0, k)
            hin[j] = total.astype(jnp.bfloat16)
            backward[j].start()

    @pl.when(p == 0)
    def _():
        launch(xg[0])

    loads[7].wait()
    for c in wx_send:
        c.start()
    wx_self.start()

    @pl.when(p == 1)
    def _():
        pl.semaphore_wait(go, 1)

    @pl.when(p > 0)
    def _():
        wait_wx()
        wo_self.start()
        for c in wo_send:
            c.start()

    def use(j, zz):
        col = (zz + NZ) % NZ
        x = xbuf[j, pl.ds(pl.multiple_of(col * NY * f, NY * f), NY * f), :]
        acc[j] += jnp.dot(wq[col], x, preferred_element_type=jnp.float32)
        xf = x.astype(jnp.float32)
        square[j] += jnp.sum(xf * xf, axis=0, keepdims=True)

    def xstage(j, i):
        stage(xg[j], i, lambda zz: use(j, zz))

    kpos = lax.broadcasted_iota(jnp.int32, (toks, toks), 0)
    qpos = lax.broadcasted_iota(jnp.int32, (toks, toks), 1)
    kframe, qframe = kpos // SPATIAL, qpos // SPATIAL

    def attention(j, whole=False):
        same_frame = kframe == qframe
        causal = (kpos % SPATIAL == qpos % SPATIAL) & (kframe <= qframe)
        seen = jnp.zeros((toks, toks), jnp.int32)
        for fr in range(FRAMES):
            seen = jnp.where(kframe == fr, vis[plan[j], fr], seen)
        temporal = jnp.where(causal & ((seen == 1) | same_frame), 1, 0)
        allowed = jnp.where(p % 2 == 0, jnp.where(same_frame, 1, 0), temporal)
        scale = lax.rsqrt(square[j] * (1.0 / (NY * NZ * f)) + 1e-05)
        qkv = (acc[j] * scale).astype(jnp.bfloat16)
        query, keys, values = qkv[:HD], qkv[HD:2 * HD], qkv[2 * HD:]
        scores = lax.dot_general(
            keys, query, (((0,), (0,)), ((), ())), preferred_element_type=jnp.float32
        ) * HD ** (-0.5)
        scores = jnp.where(allowed == 1, scores, -1e30)
        top = jnp.max(scores, axis=0, keepdims=True)
        weights = jnp.exp(scores - top)
        probs = (weights / jnp.sum(weights, axis=0, keepdims=True)).astype(jnp.bfloat16)
        attn = jnp.dot(values, probs, preferred_element_type=jnp.float32)
        if whole:
            own = pl.ds(pl.multiple_of((y * NZ + z) * HD, HD), HD)
            afull[j, own, :] = attn.astype(jnp.bfloat16)
            launch(ag[j])
            return
        abuf[j, own_a, :] = attn.astype(jnp.bfloat16)
        for k in (4, 3, 5, 2, 6, 1, 7):
            acopies[j, k].start()

    def project(j):
        for k in range(1, NZ):
            acopies[j, k].wait_recv()
        for k in (2, 1, 3, 0):
            yy = (y + k) % NY
            part = jnp.dot(wo[yy], abuf[j], preferred_element_type=jnp.float32)
            pbuf[j, yy] = part.astype(jnp.bfloat16)
            if k:
                rcopies[j, k].start()
            else:
                pacc[j] = part

        @pl.when(p < 3)
        def _():
            rcopies[j, 0].start()

    def finish_whole(j):
        total = xbuf[j, own_f, :].astype(jnp.float32)
        for yy in range(NY):
            total += jnp.dot(
                wx[yy], afull[j, yy * NZ * HD:(yy + 1) * NZ * HD, :],
                preferred_element_type=jnp.float32,
            )
        out[j] = total.astype(jnp.bfloat16)
        pipe_copies[j].start()

    def finish(j):
        @pl.when(p == 3)
        def _():
            total = xbuf[j, own_f, :].astype(jnp.float32) + pacc[j]
            for k in range(1, NY):
                total += collect(j, 1, k)
            out[j] = total.astype(jnp.bfloat16)

    @pl.when(p == 0)
    def _():
        xstage(0, 0)
        xstage(0, 1)
        launch(xg[1])
        xstage(0, 2)
        attention(0, whole=True)
        xstage(1, 0)
        stage(ag[0], 0)
        pl.semaphore_signal(go, inc=1, device_id={"pipe": 1}, device_id_type=MESH)
        xstage(1, 1)
        stage(ag[0], 1)
        xstage(1, 2)
        attention(1, whole=True)
        wait_wx()
        stage(ag[0], 2)
        finish_whole(0)
        stage(ag[1], 0)
        stage(ag[1], 1)
        stage(ag[1], 2)
        finish_whole(1)
        for first, ring in ag:
            for c in list(first.values()) + list(ring.values()):
                c.wait_send()

    @pl.when(p > 0)
    def _():
        arrive(0)
        cond(0)
        xstage(0, 0)
        xstage(0, 1)
        arrive(1)
        cond(1)
        xstage(0, 2)
        attention(0)
        xstage(1, 0)
        wait_wo()
        project(0)
        xstage(1, 1)
        finish(0)
        xstage(1, 2)
        attention(1)
        project(1)
        finish(1)
        for c in list(acopies.values()) + wo_send:
            c.wait_send()
        for j in range(2):
            for k in range(1, NY):
                rcopies[j, k].wait_send()

        @pl.when(p < 3)
        def _():
            for j in range(2):
                rcopies[j, 0].wait_send()
                onward[j].wait_send()
                backward[j].wait_recv()
                out[j] = hback[j]

        @pl.when(p >= 2)
        def _():
            for c in backward:
                c.wait_send()

    for first, ring in xg:
        for c in list(first.values()) + list(ring.values()):
            c.wait_send()
    for c in wx_send:
        c.wait_send()

    @pl.when(p == 0)
    def _():
        for c in pipe_copies:
            c.wait_send()


def shards(
    clips_in, action_ids, frame_visible, plan, qkv_weight, norm_gain, action_table, out_weight
):
    clips, toks, f = clips_in.shape
    n = qkv_weight.shape[2]
    rows = out_weight.shape[1]
    bf16 = jnp.bfloat16
    xt = jnp.swapaxes(clips_in, 1, 2)
    vmem = pl.BlockSpec(memory_space=pltpu.VMEM)
    dma = pltpu.SemaphoreType.DMA
    res = pl.pallas_call(
        kernel,
        out_shape=jax.ShapeDtypeStruct((clips, f, toks), bf16),
        in_specs=[pl.BlockSpec(memory_space=pl.ANY)] * 8,
        out_specs=vmem,
        scratch_shapes=[
            pltpu.SMEM(plan.shape, jnp.int32),
            pltpu.SMEM(action_ids.shape, jnp.int32),
            pltpu.SMEM(frame_visible.shape, jnp.int32),
            pltpu.VMEM((clips, f, toks), bf16),
            pltpu.VMEM(action_table.shape[1:], bf16),
            pltpu.VMEM(norm_gain.shape, bf16),
            pltpu.VMEM((f, rows), bf16),
            pltpu.VMEM((NY * NZ * f, n), bf16),
            pltpu.VMEM((NZ, n, NY * f), bf16),
            pltpu.VMEM((clips, f, toks), jnp.float32),
            pltpu.VMEM((clips, 1, toks), jnp.float32),
            pltpu.VMEM((clips, NY * NZ * f, toks), bf16),
            pltpu.VMEM((clips, NZ * HD, toks), bf16),
            pltpu.VMEM((clips, NY * NZ * HD, toks), bf16),
            pltpu.VMEM((NY, f, rows), bf16),
            pltpu.VMEM((NY, f, rows), bf16),
            pltpu.VMEM((clips, f, toks), bf16),
            pltpu.VMEM((clips, f, toks), bf16),
            pltpu.VMEM((clips, f, toks), bf16),
            pltpu.VMEM((clips, n, toks), jnp.float32),
            pltpu.VMEM((clips, f, toks), jnp.float32),
            pltpu.VMEM((clips, NY, f, toks), bf16),
            pltpu.VMEM((clips, 2, NY, f, toks), bf16),
            dma((2, 3)), dma((2, 3)),
            dma((2, 2, 4, 4)), dma((2, 2, 4, 4)),
            dma((2, 3)), dma((2, 3)),
            dma((2, 2, 4, 4)), dma((2, 2, 4, 4)),
            dma((2, 7)), dma((2, 7)),
            dma((2, 4)), dma((2, 2, 4)),
            dma((2,)), dma((2,)),
            dma((2,)), dma((2,)),
            dma((2,)), dma((2,)),
            dma((3,)), dma((3,)),
            dma((3,)), dma((3,)),
            dma((2,)), dma((8,)),
            pltpu.SemaphoreType.REGULAR,
        ],
        compiler_params=pltpu.CompilerParams(
            collective_id=0, has_side_effects=True, vmem_limit_bytes=63 * 1024 * 1024
        ),
    )(plan, action_ids, frame_visible, xt, action_table[0], norm_gain, qkv_weight[0], out_weight[0].T)
    return jnp.swapaxes(res, 1, 2)[None]


def solution(mesh):
    return jax.shard_map(
        shards,
        mesh=mesh,
        in_specs=(
            P("dp", None, "seq"),
            P("dp", None),
            P("dp", None),
            P(),
            P("pipe", None, "seq"),
            P("pipe", None),
            P("pipe", None, "seq"),
            P("pipe", "dp", "seq"),
        ),
        out_specs=P("pipe", "dp", None, "seq"),
        check_vma=False,
    )
```

```python
import jax
import jax.numpy as jnp
from jax import lax
from jax.experimental import pallas as pl
from jax.experimental.pallas import tpu as pltpu
from jax.sharding import PartitionSpec as P

HD = 128
SPATIAL = 16
FRAMES = 8
NY = 4
NZ = 8
MESH = pl.DeviceIdType.MESH


def kernel(
    plan_in, acts_in, vis_in, clips_in, table_in, gain_in, w_in, wo_in,
    out,
    plan, acts, vis, clips, table, gain, wo_loc, w_raw, wq, embeds, square, xbuf, abuf, afull, wx, wo, hin, cbuf, hback, acc, pacc, pbuf, rbuf,
    ysend, yrecv, zsend, zrecv, y2send, y2recv, z2send, z2recv, asend, arecv, rsend, rrecv, psend, precv, csend, crecv, bsend, brecv,
    dsend, drecv, wsend, wrecv, lsem, wsem, go,
):
    p = lax.axis_index("pipe")
    s = lax.axis_index("seq")
    d = lax.axis_index("dp")
    y = s // NZ
    z = s % NZ
    f, toks = hin.shape[1], hin.shape[2]

    def place(yy, zz):
        return {"seq": (yy % NY) * NZ + zz % NZ}

    def remote(src, dst, send_sem, recv_sem, device):
        return pltpu.make_async_remote_copy(
            src_ref=src, dst_ref=dst, send_sem=send_sem, recv_sem=recv_sem,
            device_id=device, device_id_type=MESH,
        )

    def greet(device):
        pl.semaphore_signal(barrier, inc=1, device_id=device, device_id_type=MESH)

    barrier = pltpu.get_barrier_semaphore()
    for k in range(1, NY):
        greet(place(y + k, z))
        greet({"dp": (d + k) % NY})
    for k in range(1, NZ):
        greet(place(y, z + k))
    greet({"pipe": (p + 1) % 4})
    greet({"pipe": (p + 3) % 4})
    hands_on = (p + 1) // 2 % 2

    @pl.when(p >= 2)
    def _():
        for k in range(1, NY):
            greet({"pipe": p - 1, "seq": (y + k) % NY * NZ + z})

    loads = [
        pltpu.make_async_copy(src, dst, wsem.at[i])
        for i, (src, dst) in enumerate((
            (plan_in, plan), (acts_in, acts), (clips_in, clips), (table_in, table),
            (vis_in, vis), (gain_in, gain), (w_in, w_raw), (wo_in, wo_loc),
        ))
    ]
    for c in loads:
        c.start()

    rows8 = lax.broadcasted_iota(jnp.int32, (8, toks), 0)
    lane = lax.broadcasted_iota(jnp.int32, (8, toks), 1)

    def embed(j):
        act_of = jnp.zeros((8, toks), jnp.int32)
        for fr in range(FRAMES):
            act_of = jnp.where(lane // SPATIAL == fr, acts[plan[j], fr], act_of)
        onehot = (act_of == rows8).astype(jnp.float32)
        return lax.dot_general(
            table[...].astype(jnp.float32), onehot, (((0,), (0,)), ((), ())),
            preferred_element_type=jnp.float32, precision=lax.Precision.HIGHEST,
        )

    for c in loads[:4]:
        c.wait()
    for j in range(2):
        embeds[j] = embed(j)
    own_f = pl.ds(pl.multiple_of((z * NY + y) * f, f), f)

    def condition(j, stream):
        xbuf[j, own_f, :] = (stream.astype(jnp.float32) + embeds[j]).astype(jnp.bfloat16)

    @pl.when(p == 0)
    def _():
        for j in range(2):
            condition(j, clips[plan[j]])

    for c in loads[4:7]:
        c.wait()

    def prepare(col):
        blocks = [
            w_raw[(yy * NZ + col) * f:(yy * NZ + col + 1) * f, :] for yy in range(NY)
        ]
        w = jnp.concatenate(blocks, axis=0).T
        g = [gain[:, (yy * NZ + col) * f:(yy * NZ + col + 1) * f] for yy in range(NY)]
        g = jnp.concatenate(g, axis=1).astype(jnp.float32)
        wq[col] = (w.astype(jnp.float32) * g).astype(jnp.bfloat16)

    for col in range(NZ):
        prepare(col)

    pl.semaphore_wait(barrier, 2 * (NY - 1) + NZ - 1 + 2 + (NY - 1) * hands_on)

    wx_self = pltpu.make_async_copy(wo_loc, wx.at[d], lsem.at[0])
    wx_send = [
        remote(wo_loc, wx.at[d], dsend.at[k - 1], drecv.at[k - 1], {"dp": (d + k) % NY})
        for k in range(1, NY)
    ]
    wo_self = pltpu.make_async_copy(wx.at[y], wo.at[y], lsem.at[1])
    wo_send = [
        remote(wx.at[(y + k) % NY], wo.at[y], wsend.at[k - 1], wrecv.at[k - 1], place(y + k, z))
        for k in range(1, NY)
    ]

    def wait_wx():
        wx_self.wait()
        for c in wx_send:
            c.wait_recv()

    def wait_wo():
        wo_self.wait()
        for c in wo_send:
            c.wait_recv()

    pipe_copies = [
        remote(out.at[j], hin.at[j], psend.at[j], precv.at[j], {"pipe": (p + 1) % 4})
        for j in range(2)
    ]
    def block(j, yy, zz):
        row = ((zz + NZ) % NZ * NY + (yy + NY) % NY) * f
        return xbuf.at[j, pl.ds(pl.multiple_of(row, f), f), :]

    def block_a(j, yy, zz):
        row = ((yy + NY) % NY * NZ + (zz + NZ) % NZ) * HD
        return afull.at[j, pl.ds(pl.multiple_of(row, HD), HD), :]

    def plan_gather(j, piece, y_send, y_recv, z_send, z_recv):
        first, ring = {}, {}
        for k in range(1, NY):
            ref = piece(j, y, z)
            first[k] = remote(ref, ref, y_send.at[j, k - 1], y_recv.at[j, k - 1], place(y + k, z))
        for k in range(NY):
            for way in range(2):
                for dist in range(1, 5):
                    if dist == 4 and (k < 2) != (way == 0):
                        continue
                    hop = {1: 1, 2: 2, 3: 1, 4: 2}[dist]
                    back = dist - hop
                    ref = piece(j, y - k, z + back if way else z - back)
                    ring[way, dist, k] = remote(
                        ref, ref, z_send.at[j, way, dist - 1, k], z_recv.at[j, way, dist - 1, k],
                        place(y, z + NZ - hop if way else z + hop),
                    )
        return first, ring

    xg = [plan_gather(j, block, ysend, yrecv, zsend, zrecv) for j in range(2)]
    ag = [plan_gather(j, block_a, y2send, y2recv, z2send, z2recv) for j in range(2)]
    acopies, rcopies = {}, {}
    onward = [
        remote(xbuf.at[j, own_f, :], cbuf.at[j], csend.at[j], crecv.at[j], {"pipe": (p + 1) % 4})
        for j in range(2)
    ]
    backward = [
        remote(hin.at[j], hback.at[j], bsend.at[j], brecv.at[j], {"pipe": (p + 3) % 4})
        for j in range(2)
    ]
    own_a = pl.ds(pl.multiple_of(z * HD, HD), HD)
    for j in range(2):
        for k in range(NY):
            rcopies[j, k] = remote(
                pbuf.at[j, (y + k) % NY], rbuf.at[j, p // 3, k],
                rsend.at[j, k], rrecv.at[j, p // 3, k],
                {"pipe": p + 1 - p // 3, "seq": (y + k) % NY * NZ + z},
            )
        for k in range(1, NZ):
            ref = abuf.at[j, own_a, :]
            acopies[j, k] = remote(
                ref, ref, asend.at[j, k - 1], arecv.at[j, k - 1], place(y, z + k)
            )

    def launch(gather):
        first, ring = gather
        for k in (1, 3, 2):
            first[k].start()
        for dist in (2, 1):
            for way in range(2):
                ring[way, dist, 0].start()

    def stage(gather, i, use=None):
        first, ring = gather
        if i == 0:
            for k in (1, 3, 2):
                first[k].wait_recv()
                for way in range(2):
                    ring[way, 2, k].start()
            for k in range(1, NY):
                for way in range(2):
                    ring[way, 1, k].start()
            if use:
                use(z)
        if i == 1:
            for k in (0, 1, 3, 2):
                for way in range(2):
                    ring[way, 2, k].wait_recv()
                    if (k < 2) == (way == 0):
                        ring[way, 4, k].start()
                    ring[way, 3, k].start()
            if use:
                use(z - 2)
                use(z + 2)
            for k in range(NY):
                for way in range(2):
                    ring[way, 1, k].wait_recv()
            if use:
                use(z - 1)
                use(z + 1)
        if i == 2:
            for k in range(NY):
                for way in range(2):
                    ring[way, 3, k].wait_recv()
            if use:
                use(z - 3)
                use(z + 3)
            for k in range(NY):
                ring[0 if k < 2 else 1, 4, k].wait_recv()
            if use:
                use(z + 4)

    def cond(j):
        condition(j, hin[j])
        launch(xg[j])

        @pl.when(hands_on == 1)
        def _():
            onward[j].start()

    for j in range(2):
        acc[j] = jnp.zeros_like(acc[j])
        square[j] = jnp.zeros_like(square[j])

    def collect(j, g, k):
        pltpu.make_async_copy(pbuf.at[j, 0], rbuf.at[j, g, k], rrecv.at[j, g, k]).wait()
        return rbuf[j, g, k].astype(jnp.float32)

    def arrive(j):
        @pl.when(p == 1)
        def _():
            pipe_copies[j].wait_recv()

        @pl.when(p >= 2)
        def _():
            onward[j].wait_recv()
            total = cbuf[j].astype(jnp.float32)
            for k in range(NY):
                total += collect(j, 0, k)
            hin[j] = total.astype(jnp.bfloat16)
            backward[j].start()

    @pl.when(p == 0)
    def _():
        launch(xg[0])

    loads[7].wait()
    for c in wx_send:
        c.start()
    wx_self.start()

    @pl.when(p == 1)
    def _():
        pl.semaphore_wait(go, 1)

    @pl.when(p > 0)
    def _():
        wait_wx()
        wo_self.start()
        for c in wo_send:
            c.start()

    def use(j, zz):
        col = (zz + NZ) % NZ
        x = xbuf[j, pl.ds(pl.multiple_of(col * NY * f, NY * f), NY * f), :]
        acc[j] += jnp.dot(wq[col], x, preferred_element_type=jnp.float32)
        xf = x.astype(jnp.float32)
        square[j] += jnp.sum(xf * xf, axis=0, keepdims=True)

    def xstage(j, i):
        stage(xg[j], i, lambda zz: use(j, zz))

    kpos = lax.broadcasted_iota(jnp.int32, (toks, toks), 0)
    qpos = lax.broadcasted_iota(jnp.int32, (toks, toks), 1)
    kframe, qframe = kpos // SPATIAL, qpos // SPATIAL

    def attention(j, whole=False):
        same_frame = kframe == qframe
        causal = (kpos % SPATIAL == qpos % SPATIAL) & (kframe <= qframe)
        seen = jnp.zeros((toks, toks), jnp.int32)
        for fr in range(FRAMES):
            seen = jnp.where(kframe == fr, vis[plan[j], fr], seen)
        temporal = jnp.where(causal & ((seen == 1) | same_frame), 1, 0)
        allowed = jnp.where(p % 2 == 0, jnp.where(same_frame, 1, 0), temporal)
        scale = lax.rsqrt(square[j] * (1.0 / (NY * NZ * f)) + 1e-05)
        qkv = (acc[j] * scale).astype(jnp.bfloat16)
        query, keys, values = qkv[:HD], qkv[HD:2 * HD], qkv[2 * HD:]
        scores = lax.dot_general(
            keys, query, (((0,), (0,)), ((), ())), preferred_element_type=jnp.float32
        ) * HD ** (-0.5)
        scores = jnp.where(allowed == 1, scores, -1e30)
        top = jnp.max(scores, axis=0, keepdims=True)
        weights = jnp.exp(scores - top)
        probs = (weights / jnp.sum(weights, axis=0, keepdims=True)).astype(jnp.bfloat16)
        attn = jnp.dot(values, probs, preferred_element_type=jnp.float32)
        if whole:
            own = pl.ds(pl.multiple_of((y * NZ + z) * HD, HD), HD)
            afull[j, own, :] = attn.astype(jnp.bfloat16)
            launch(ag[j])
            return
        abuf[j, own_a, :] = attn.astype(jnp.bfloat16)
        for k in (4, 3, 5, 2, 6, 1, 7):
            acopies[j, k].start()

    def project(j):
        for k in range(1, NZ):
            acopies[j, k].wait_recv()
        for k in (2, 1, 3, 0):
            yy = (y + k) % NY
            part = jnp.dot(wo[yy], abuf[j], preferred_element_type=jnp.float32)
            pbuf[j, yy] = part.astype(jnp.bfloat16)
            if k:
                rcopies[j, k].start()
            else:
                pacc[j] = part

        @pl.when(p < 3)
        def _():
            rcopies[j, 0].start()

    def finish_whole(j):
        total = xbuf[j, own_f, :].astype(jnp.float32)
        for yy in range(NY):
            total += jnp.dot(
                wx[yy], afull[j, yy * NZ * HD:(yy + 1) * NZ * HD, :],
                preferred_element_type=jnp.float32,
            )
        out[j] = total.astype(jnp.bfloat16)
        pipe_copies[j].start()

    def finish(j):
        @pl.when(p == 3)
        def _():
            total = xbuf[j, own_f, :].astype(jnp.float32) + pacc[j]
            for k in range(1, NY):
                total += collect(j, 1, k)
            out[j] = total.astype(jnp.bfloat16)

    @pl.when(p == 0)
    def _():
        xstage(0, 0)
        xstage(0, 1)
        launch(xg[1])
        xstage(0, 2)
        attention(0, whole=True)
        xstage(1, 0)
        stage(ag[0], 0)
        pl.semaphore_signal(go, inc=1, device_id={"pipe": 1}, device_id_type=MESH)
        xstage(1, 1)
        stage(ag[0], 1)
        xstage(1, 2)
        attention(1, whole=True)
        wait_wx()
        stage(ag[0], 2)
        finish_whole(0)
        stage(ag[1], 0)
        stage(ag[1], 1)
        stage(ag[1], 2)
        finish_whole(1)
        for first, ring in ag:
            for c in list(first.values()) + list(ring.values()):
                c.wait_send()

    @pl.when(p > 0)
    def _():
        arrive(0)
        cond(0)
        xstage(0, 0)
        xstage(0, 1)
        arrive(1)
        cond(1)
        xstage(0, 2)
        attention(0)
        xstage(1, 0)
        wait_wo()
        project(0)
        xstage(1, 1)
        finish(0)
        xstage(1, 2)
        attention(1)
        project(1)
        finish(1)
        for c in list(acopies.values()) + wo_send:
            c.wait_send()
        for j in range(2):
            for k in range(1, NY):
                rcopies[j, k].wait_send()

        @pl.when(p < 3)
        def _():
            for j in range(2):
                rcopies[j, 0].wait_send()
                onward[j].wait_send()
                backward[j].wait_recv()
                out[j] = hback[j]

        @pl.when(p >= 2)
        def _():
            for c in backward:
                c.wait_send()

    for first, ring in xg:
        for c in list(first.values()) + list(ring.values()):
            c.wait_send()
    for c in wx_send:
        c.wait_send()

    @pl.when(p == 0)
    def _():
        for c in pipe_copies:
            c.wait_send()


def shards(
    clips_in, action_ids, frame_visible, plan, qkv_weight, norm_gain, action_table, out_weight
):
    clips, toks, f = clips_in.shape
    n = qkv_weight.shape[2]
    rows = out_weight.shape[1]
    bf16 = jnp.bfloat16
    xt = jnp.swapaxes(clips_in, 1, 2)
    vmem = pl.BlockSpec(memory_space=pltpu.VMEM)
    dma = pltpu.SemaphoreType.DMA
    res = pl.pallas_call(
        kernel,
        out_shape=jax.ShapeDtypeStruct((clips, f, toks), bf16),
        in_specs=[pl.BlockSpec(memory_space=pl.ANY)] * 8,
        out_specs=vmem,
        scratch_shapes=[
            pltpu.SMEM(plan.shape, jnp.int32),
            pltpu.SMEM(action_ids.shape, jnp.int32),
            pltpu.SMEM(frame_visible.shape, jnp.int32),
            pltpu.VMEM((clips, f, toks), bf16),
            pltpu.VMEM(action_table.shape[1:], bf16),
            pltpu.VMEM(norm_gain.shape, bf16),
            pltpu.VMEM((f, rows), bf16),
            pltpu.VMEM((NY * NZ * f, n), bf16),
            pltpu.VMEM((NZ, n, NY * f), bf16),
            pltpu.VMEM((clips, f, toks), jnp.float32),
            pltpu.VMEM((clips, 1, toks), jnp.float32),
            pltpu.VMEM((clips, NY * NZ * f, toks), bf16),
            pltpu.VMEM((clips, NZ * HD, toks), bf16),
            pltpu.VMEM((clips, NY * NZ * HD, toks), bf16),
            pltpu.VMEM((NY, f, rows), bf16),
            pltpu.VMEM((NY, f, rows), bf16),
            pltpu.VMEM((clips, f, toks), bf16),
            pltpu.VMEM((clips, f, toks), bf16),
            pltpu.VMEM((clips, f, toks), bf16),
            pltpu.VMEM((clips, n, toks), jnp.float32),
            pltpu.VMEM((clips, f, toks), jnp.float32),
            pltpu.VMEM((clips, NY, f, toks), bf16),
            pltpu.VMEM((clips, 2, NY, f, toks), bf16),
            dma((2, 3)), dma((2, 3)),
            dma((2, 2, 4, 4)), dma((2, 2, 4, 4)),
            dma((2, 3)), dma((2, 3)),
            dma((2, 2, 4, 4)), dma((2, 2, 4, 4)),
            dma((2, 7)), dma((2, 7)),
            dma((2, 4)), dma((2, 2, 4)),
            dma((2,)), dma((2,)),
            dma((2,)), dma((2,)),
            dma((2,)), dma((2,)),
            dma((3,)), dma((3,)),
            dma((3,)), dma((3,)),
            dma((2,)), dma((8,)),
            pltpu.SemaphoreType.REGULAR,
        ],
        compiler_params=pltpu.CompilerParams(
            collective_id=0, has_side_effects=True, vmem_limit_bytes=63 * 1024 * 1024
        ),
    )(plan, action_ids, frame_visible, xt, action_table[0], norm_gain, qkv_weight[0], out_weight[0].T)
    return jnp.swapaxes(res, 1, 2)[None]


def solution(mesh):
    return jax.shard_map(
        shards,
        mesh=mesh,
        in_specs=(
            P("dp", None, "seq"),
            P("dp", None),
            P("dp", None),
            P(),
            P("pipe", None, "seq"),
            P("pipe", None),
            P("pipe", None, "seq"),
            P("pipe", "dp", "seq"),
        ),
        out_specs=P("pipe", "dp", None, "seq"),
        check_vma=False,
    )
```

```python
import jax
import jax.numpy as jnp
from jax import lax
from jax.experimental import pallas as pl
from jax.experimental.pallas import tpu as pltpu
from jax.sharding import PartitionSpec as P

HD = 128
SPATIAL = 16
FRAMES = 8
NY = 4
NZ = 8
MESH = pl.DeviceIdType.MESH


def kernel(
    plan_in, acts_in, vis_in, clips_in, table_in, gain_in, w_in, wo_in,
    out,
    plan, acts, vis, clips, table, gain, wo_loc, w_raw, wq, embeds, square, xbuf, abuf, afull, wx, wo, hin, cbuf, hback, acc, pacc, pbuf, rbuf,
    ysend, yrecv, zsend, zrecv, y2send, y2recv, z2send, z2recv, asend, arecv, rsend, rrecv, psend, precv, csend, crecv, bsend, brecv,
    dsend, drecv, wsend, wrecv, lsem, wsem, go,
):
    p = lax.axis_index("pipe")
    s = lax.axis_index("seq")
    d = lax.axis_index("dp")
    y = s // NZ
    z = s % NZ
    f, toks = hin.shape[1], hin.shape[2]

    def place(yy, zz):
        return {"seq": (yy % NY) * NZ + zz % NZ}

    def remote(src, dst, send_sem, recv_sem, device):
        return pltpu.make_async_remote_copy(
            src_ref=src, dst_ref=dst, send_sem=send_sem, recv_sem=recv_sem,
            device_id=device, device_id_type=MESH,
        )

    def greet(device):
        pl.semaphore_signal(barrier, inc=1, device_id=device, device_id_type=MESH)

    barrier = pltpu.get_barrier_semaphore()
    for k in range(1, NY):
        greet(place(y + k, z))
        greet({"dp": (d + k) % NY})
    for k in range(1, NZ):
        greet(place(y, z + k))
    greet({"pipe": (p + 1) % 4})
    greet({"pipe": (p + 3) % 4})
    hands_on = (p + 1) // 2 % 2

    @pl.when(p >= 2)
    def _():
        for k in range(1, NY):
            greet({"pipe": p - 1, "seq": (y + k) % NY * NZ + z})

    loads = [
        pltpu.make_async_copy(src, dst, wsem.at[i])
        for i, (src, dst) in enumerate((
            (plan_in, plan), (acts_in, acts), (clips_in, clips), (table_in, table),
            (vis_in, vis), (gain_in, gain), (w_in, w_raw), (wo_in, wo_loc),
        ))
    ]
    for c in loads:
        c.start()

    rows8 = lax.broadcasted_iota(jnp.int32, (8, toks), 0)
    lane = lax.broadcasted_iota(jnp.int32, (8, toks), 1)

    def embed(j):
        act_of = jnp.zeros((8, toks), jnp.int32)
        for fr in range(FRAMES):
            act_of = jnp.where(lane // SPATIAL == fr, acts[plan[j], fr], act_of)
        onehot = (act_of == rows8).astype(jnp.float32)
        return lax.dot_general(
            table[...].astype(jnp.float32), onehot, (((0,), (0,)), ((), ())),
            preferred_element_type=jnp.float32, precision=lax.Precision.HIGHEST,
        )

    for c in loads[:4]:
        c.wait()
    for j in range(2):
        embeds[j] = embed(j)
    own_f = pl.ds(pl.multiple_of((z * NY + y) * f, f), f)

    def condition(j, stream):
        xbuf[j, own_f, :] = (stream.astype(jnp.float32) + embeds[j]).astype(jnp.bfloat16)

    @pl.when(p == 0)
    def _():
        for j in range(2):
            condition(j, clips[plan[j]])

    for c in loads[4:7]:
        c.wait()

    def prepare(col):
        blocks = [
            w_raw[(yy * NZ + col) * f:(yy * NZ + col + 1) * f, :] for yy in range(NY)
        ]
        w = jnp.concatenate(blocks, axis=0).T
        g = [gain[:, (yy * NZ + col) * f:(yy * NZ + col + 1) * f] for yy in range(NY)]
        g = jnp.concatenate(g, axis=1).astype(jnp.float32)
        wq[col] = (w.astype(jnp.float32) * g).astype(jnp.bfloat16)

    for col in range(NZ):
        prepare(col)

    pl.semaphore_wait(barrier, 2 * (NY - 1) + NZ - 1 + 2 + (NY - 1) * hands_on)

    wx_self = pltpu.make_async_copy(wo_loc, wx.at[d], lsem.at[0])
    wx_send = [
        remote(wo_loc, wx.at[d], dsend.at[k - 1], drecv.at[k - 1], {"dp": (d + k) % NY})
        for k in range(1, NY)
    ]
    wo_self = pltpu.make_async_copy(wx.at[y], wo.at[y], lsem.at[1])
    wo_send = [
        remote(wx.at[(y + k) % NY], wo.at[y], wsend.at[k - 1], wrecv.at[k - 1], place(y + k, z))
        for k in range(1, NY)
    ]

    def wait_wx():
        wx_self.wait()
        for c in wx_send:
            c.wait_recv()

    def wait_wo():
        wo_self.wait()
        for c in wo_send:
            c.wait_recv()

    pipe_copies = [
        remote(out.at[j], hin.at[j], psend.at[j], precv.at[j], {"pipe": (p + 1) % 4})
        for j in range(2)
    ]
    def block(j, yy, zz):
        row = ((zz + NZ) % NZ * NY + (yy + NY) % NY) * f
        return xbuf.at[j, pl.ds(pl.multiple_of(row, f), f), :]

    def block_a(j, yy, zz):
        row = ((yy + NY) % NY * NZ + (zz + NZ) % NZ) * HD
        return afull.at[j, pl.ds(pl.multiple_of(row, HD), HD), :]

    def plan_gather(j, piece, y_send, y_recv, z_send, z_recv):
        first, ring = {}, {}
        for k in range(1, NY):
            ref = piece(j, y, z)
            first[k] = remote(ref, ref, y_send.at[j, k - 1], y_recv.at[j, k - 1], place(y + k, z))
        for k in range(NY):
            for way in range(2):
                for dist in range(1, 5):
                    if dist == 4 and (k < 2) != (way == 0):
                        continue
                    hop = {1: 1, 2: 2, 3: 1, 4: 2}[dist]
                    back = dist - hop
                    ref = piece(j, y - k, z + back if way else z - back)
                    ring[way, dist, k] = remote(
                        ref, ref, z_send.at[j, way, dist - 1, k], z_recv.at[j, way, dist - 1, k],
                        place(y, z + NZ - hop if way else z + hop),
                    )
        return first, ring

    xg = [plan_gather(j, block, ysend, yrecv, zsend, zrecv) for j in range(2)]
    ag = [plan_gather(j, block_a, y2send, y2recv, z2send, z2recv) for j in range(2)]
    acopies, rcopies = {}, {}
    onward = [
        remote(xbuf.at[j, own_f, :], cbuf.at[j], csend.at[j], crecv.at[j], {"pipe": (p + 1) % 4})
        for j in range(2)
    ]
    backward = [
        remote(hin.at[j], hback.at[j], bsend.at[j], brecv.at[j], {"pipe": (p + 3) % 4})
        for j in range(2)
    ]
    own_a = pl.ds(pl.multiple_of(z * HD, HD), HD)
    for j in range(2):
        for k in range(NY):
            rcopies[j, k] = remote(
                pbuf.at[j, (y + k) % NY], rbuf.at[j, p // 3, k],
                rsend.at[j, k], rrecv.at[j, p // 3, k],
                {"pipe": p + 1 - p // 3, "seq": (y + k) % NY * NZ + z},
            )
        for k in range(1, NZ):
            ref = abuf.at[j, own_a, :]
            acopies[j, k] = remote(
                ref, ref, asend.at[j, k - 1], arecv.at[j, k - 1], place(y, z + k)
            )

    def launch(gather):
        first, ring = gather
        for k in (1, 3, 2):
            first[k].start()
        for dist in (2, 1):
            for way in range(2):
                ring[way, dist, 0].start()

    def stage(gather, i, use=None):
        first, ring = gather
        if i == 0:
            for k in (1, 3, 2):
                first[k].wait_recv()
                for way in range(2):
                    ring[way, 2, k].start()
            for k in range(1, NY):
                for way in range(2):
                    ring[way, 1, k].start()
            if use:
                use(z)
        if i == 1:
            for k in (0, 1, 3, 2):
                for way in range(2):
                    ring[way, 2, k].wait_recv()
                    if (k < 2) == (way == 0):
                        ring[way, 4, k].start()
                    ring[way, 3, k].start()
            if use:
                use(z - 2)
                use(z + 2)
            for k in range(NY):
                for way in range(2):
                    ring[way, 1, k].wait_recv()
            if use:
                use(z - 1)
                use(z + 1)
        if i == 2:
            for k in range(NY):
                for way in range(2):
                    ring[way, 3, k].wait_recv()
            if use:
                use(z - 3)
                use(z + 3)
            for k in range(NY):
                ring[0 if k < 2 else 1, 4, k].wait_recv()
            if use:
                use(z + 4)

    def cond(j):
        condition(j, hin[j])
        launch(xg[j])

        @pl.when(hands_on == 1)
        def _():
            onward[j].start()

    for j in range(2):
        acc[j] = jnp.zeros_like(acc[j])
        square[j] = jnp.zeros_like(square[j])

    def collect(j, g, k):
        pltpu.make_async_copy(pbuf.at[j, 0], rbuf.at[j, g, k], rrecv.at[j, g, k]).wait()
        return rbuf[j, g, k].astype(jnp.float32)

    def arrive(j):
        @pl.when(p == 1)
        def _():
            pipe_copies[j].wait_recv()

        @pl.when(p >= 2)
        def _():
            onward[j].wait_recv()
            total = cbuf[j].astype(jnp.float32)
            for k in range(NY):
                total += collect(j, 0, k)
            hin[j] = total.astype(jnp.bfloat16)
            backward[j].start()

    @pl.when(p == 0)
    def _():
        launch(xg[0])

    loads[7].wait()
    for c in wx_send:
        c.start()
    wx_self.start()

    @pl.when(p == 1)
    def _():
        pl.semaphore_wait(go, 1)

    @pl.when(p > 0)
    def _():
        wait_wx()
        wo_self.start()
        for c in wo_send:
            c.start()

    def use(j, zz):
        col = (zz + NZ) % NZ
        x = xbuf[j, pl.ds(pl.multiple_of(col * NY * f, NY * f), NY * f), :]
        acc[j] += jnp.dot(wq[col], x, preferred_element_type=jnp.float32)
        xf = x.astype(jnp.float32)
        square[j] += jnp.sum(xf * xf, axis=0, keepdims=True)

    def xstage(j, i):
        stage(xg[j], i, lambda zz: use(j, zz))

    kpos = lax.broadcasted_iota(jnp.int32, (toks, toks), 0)
    qpos = lax.broadcasted_iota(jnp.int32, (toks, toks), 1)
    kframe, qframe = kpos // SPATIAL, qpos // SPATIAL

    def attention(j, whole=False):
        same_frame = kframe == qframe
        causal = (kpos % SPATIAL == qpos % SPATIAL) & (kframe <= qframe)
        seen = jnp.zeros((toks, toks), jnp.int32)
        for fr in range(FRAMES):
            seen = jnp.where(kframe == fr, vis[plan[j], fr], seen)
        temporal = jnp.where(causal & ((seen == 1) | same_frame), 1, 0)
        allowed = jnp.where(p % 2 == 0, jnp.where(same_frame, 1, 0), temporal)
        scale = lax.rsqrt(square[j] * (1.0 / (NY * NZ * f)) + 1e-05)
        qkv = (acc[j] * scale).astype(jnp.bfloat16)
        query, keys, values = qkv[:HD], qkv[HD:2 * HD], qkv[2 * HD:]
        scores = lax.dot_general(
            keys, query, (((0,), (0,)), ((), ())), preferred_element_type=jnp.float32
        ) * HD ** (-0.5)
        scores = jnp.where(allowed == 1, scores, -1e30)
        top = jnp.max(scores, axis=0, keepdims=True)
        weights = jnp.exp(scores - top)
        probs = (weights / jnp.sum(weights, axis=0, keepdims=True)).astype(jnp.bfloat16)
        attn = jnp.dot(values, probs, preferred_element_type=jnp.float32)
        if whole:
            own = pl.ds(pl.multiple_of((y * NZ + z) * HD, HD), HD)
            afull[j, own, :] = attn.astype(jnp.bfloat16)
            launch(ag[j])
            return
        abuf[j, own_a, :] = attn.astype(jnp.bfloat16)
        for k in (4, 3, 5, 2, 6, 1, 7):
            acopies[j, k].start()

    def project(j):
        for k in range(1, NZ):
            acopies[j, k].wait_recv()
        for k in (1, 3, 2, 0):
            yy = (y + k) % NY
            part = jnp.dot(wo[yy], abuf[j], preferred_element_type=jnp.float32)
            pbuf[j, yy] = part.astype(jnp.bfloat16)
            if k:
                rcopies[j, k].start()
            else:
                pacc[j] = part

        @pl.when(p < 3)
        def _():
            rcopies[j, 0].start()

    def finish_whole(j):
        total = xbuf[j, own_f, :].astype(jnp.float32)
        for yy in range(NY):
            total += jnp.dot(
                wx[yy], afull[j, yy * NZ * HD:(yy + 1) * NZ * HD, :],
                preferred_element_type=jnp.float32,
            )
        out[j] = total.astype(jnp.bfloat16)
        pipe_copies[j].start()

    def finish(j):
        @pl.when(p == 3)
        def _():
            total = xbuf[j, own_f, :].astype(jnp.float32) + pacc[j]
            for k in range(1, NY):
                total += collect(j, 1, k)
            out[j] = total.astype(jnp.bfloat16)

    @pl.when(p == 0)
    def _():
        xstage(0, 0)
        xstage(0, 1)
        launch(xg[1])
        xstage(0, 2)
        attention(0, whole=True)
        xstage(1, 0)
        stage(ag[0], 0)
        pl.semaphore_signal(go, inc=1, device_id={"pipe": 1}, device_id_type=MESH)
        xstage(1, 1)
        stage(ag[0], 1)
        xstage(1, 2)
        attention(1, whole=True)
        wait_wx()
        stage(ag[0], 2)
        finish_whole(0)
        stage(ag[1], 0)
        stage(ag[1], 1)
        stage(ag[1], 2)
        finish_whole(1)
        for first, ring in ag:
            for c in list(first.values()) + list(ring.values()):
                c.wait_send()

    @pl.when(p > 0)
    def _():
        arrive(0)
        cond(0)
        xstage(0, 0)
        xstage(0, 1)
        arrive(1)
        cond(1)
        xstage(0, 2)
        attention(0)
        xstage(1, 0)
        wait_wo()
        project(0)
        xstage(1, 1)
        finish(0)
        xstage(1, 2)
        attention(1)
        project(1)
        finish(1)
        for c in list(acopies.values()) + wo_send:
            c.wait_send()
        for j in range(2):
            for k in range(1, NY):
                rcopies[j, k].wait_send()

        @pl.when(p < 3)
        def _():
            for j in range(2):
                rcopies[j, 0].wait_send()
                onward[j].wait_send()
                backward[j].wait_recv()
                out[j] = hback[j]

        @pl.when(p >= 2)
        def _():
            for c in backward:
                c.wait_send()

    for first, ring in xg:
        for c in list(first.values()) + list(ring.values()):
            c.wait_send()
    for c in wx_send:
        c.wait_send()

    @pl.when(p == 0)
    def _():
        for c in pipe_copies:
            c.wait_send()


def shards(
    clips_in, action_ids, frame_visible, plan, qkv_weight, norm_gain, action_table, out_weight
):
    clips, toks, f = clips_in.shape
    n = qkv_weight.shape[2]
    rows = out_weight.shape[1]
    bf16 = jnp.bfloat16
    xt = jnp.swapaxes(clips_in, 1, 2)
    vmem = pl.BlockSpec(memory_space=pltpu.VMEM)
    dma = pltpu.SemaphoreType.DMA
    res = pl.pallas_call(
        kernel,
        out_shape=jax.ShapeDtypeStruct((clips, f, toks), bf16),
        in_specs=[pl.BlockSpec(memory_space=pl.ANY)] * 8,
        out_specs=vmem,
        scratch_shapes=[
            pltpu.SMEM(plan.shape, jnp.int32),
            pltpu.SMEM(action_ids.shape, jnp.int32),
            pltpu.SMEM(frame_visible.shape, jnp.int32),
            pltpu.VMEM((clips, f, toks), bf16),
            pltpu.VMEM(action_table.shape[1:], bf16),
            pltpu.VMEM(norm_gain.shape, bf16),
            pltpu.VMEM((f, rows), bf16),
            pltpu.VMEM((NY * NZ * f, n), bf16),
            pltpu.VMEM((NZ, n, NY * f), bf16),
            pltpu.VMEM((clips, f, toks), jnp.float32),
            pltpu.VMEM((clips, 1, toks), jnp.float32),
            pltpu.VMEM((clips, NY * NZ * f, toks), bf16),
            pltpu.VMEM((clips, NZ * HD, toks), bf16),
            pltpu.VMEM((clips, NY * NZ * HD, toks), bf16),
            pltpu.VMEM((NY, f, rows), bf16),
            pltpu.VMEM((NY, f, rows), bf16),
            pltpu.VMEM((clips, f, toks), bf16),
            pltpu.VMEM((clips, f, toks), bf16),
            pltpu.VMEM((clips, f, toks), bf16),
            pltpu.VMEM((clips, n, toks), jnp.float32),
            pltpu.VMEM((clips, f, toks), jnp.float32),
            pltpu.VMEM((clips, NY, f, toks), bf16),
            pltpu.VMEM((clips, 2, NY, f, toks), bf16),
            dma((2, 3)), dma((2, 3)),
            dma((2, 2, 4, 4)), dma((2, 2, 4, 4)),
            dma((2, 3)), dma((2, 3)),
            dma((2, 2, 4, 4)), dma((2, 2, 4, 4)),
            dma((2, 7)), dma((2, 7)),
            dma((2, 4)), dma((2, 2, 4)),
            dma((2,)), dma((2,)),
            dma((2,)), dma((2,)),
            dma((2,)), dma((2,)),
            dma((3,)), dma((3,)),
            dma((3,)), dma((3,)),
            dma((2,)), dma((8,)),
            pltpu.SemaphoreType.REGULAR,
        ],
        compiler_params=pltpu.CompilerParams(
            collective_id=0, has_side_effects=True, vmem_limit_bytes=63 * 1024 * 1024
        ),
    )(plan, action_ids, frame_visible, xt, action_table[0], norm_gain, qkv_weight[0], out_weight[0].T)
    return jnp.swapaxes(res, 1, 2)[None]


def solution(mesh):
    return jax.shard_map(
        shards,
        mesh=mesh,
        in_specs=(
            P("dp", None, "seq"),
            P("dp", None),
            P("dp", None),
            P(),
            P("pipe", None, "seq"),
            P("pipe", None),
            P("pipe", None, "seq"),
            P("pipe", "dp", "seq"),
        ),
        out_specs=P("pipe", "dp", None, "seq"),
        check_vma=False,
    )
```
